512 devices in a mesh: dp: 64 (over y, z), tensor: 8 (over x, core).
Axes of the slice: x: 4, y: 8, z: 8, core: 2. Of those that a mesh axis runs over, the one named last changes fastest.
Arguments:
- acts: bfloat16 [131072, 1024], P(('dp', 'tensor')), may hold values from -6 to 6
- grads_out: bfloat16 [131072, 4096], P('dp', 'tensor'), may hold values from -0.125 to 0.125
- error_buffer: bfloat16 [64, 1024, 4096], P('dp', None, 'tensor'), may hold values from -3 to 3
- prior_q: bfloat16 [4096, 32], P('tensor'), may hold values from -6 to 6
Outputs:
- residual: bfloat16 [64, 1024, 4096], P('dp', None, 'tensor')
- p_basis: float32 [1024, 32], replicated
- q_factor: float32 [4096, 32], P('tensor')
The draws below stay inside these ranges and needn't reach their ends.
All inputs are finite; a program needn't handle non-finite values.
Results may differ from the reference program's by a relative error of at most 0.001.
Values may be sent and summed in bfloat16 or wider, within the bound.
No kernel may reach another device: no remote copies, remote signals or barrier semaphores. Data moves between devices by JAX's collectives and lax.ppermute only.
A program may use at most 64 MiB of HBM per device.

```python
import jax
import jax.numpy as jnp
from jax import lax

D = 1024
FF = 4096
R = 32
REPLICAS = 64
TOK_REP = 2048
TOKENS = 131072


def levels(own_key, shape, split, smallest, high):
    def one(dim, blocks):
        heights = jax.random.uniform(jax.random.fold_in(jax.random.fold_in(own_key, 6), dim), (blocks,), jnp.float32, smallest / len(split), high / len(split))
        return jnp.repeat(jnp.exp(heights), shape[dim] // blocks).reshape((-1,) + (1,) * (len(shape) - dim - 1))

    loudness = one(*split[0])
    for cut in split[1:]:
        loudness = loudness * one(*cut)
    return loudness


def centred(stream_key, shape, spread, bound, shards=(), kind=jnp.bfloat16):
    values = jax.random.normal(stream_key, shape, jnp.float32) * spread
    if len(shards) > 0:
        values = levels(stream_key, shape, shards, -0.22, 0.18) * values
    return jnp.clip(values, min=-bound, max=bound).astype(kind)


def setup_inputs(seed: int = 0) -> dict:
    seeds = jax.random.split(jax.random.key(seed), 5)
    acts = centred(seeds[0], (TOKENS, D), 1.0, 6.0, ((0, 512),))
    grads_out = centred(seeds[1], (TOKENS, FF), TOK_REP ** -0.5, 0.125, ((0, 64), (1, 8)))
    error_buffer = centred(seeds[2], (REPLICAS, D, FF), 0.5, 3.0, ((0, 64), (2, 8)))
    prior_q = centred(seeds[3], (FF, R), 1.0, 6.0, ((0, 8),))
    return {"acts": acts, "grads_out": grads_out, "error_buffer": error_buffer, "prior_q": prior_q}


def reference(acts, grads_out, error_buffer, prior_q):
    rows = acts.reshape(REPLICAS, TOK_REP, D)
    outs = grads_out.reshape(REPLICAS, TOK_REP, FF)
    q_full = prior_q.astype(jnp.float32)
    high = lax.Precision.HIGHEST

    def merged_of(index):
        grad = jnp.dot(rows[index].T.astype(jnp.float32), outs[index].astype(jnp.float32), preferred_element_type=jnp.float32)
        return grad + error_buffer[index].astype(jnp.float32)

    def left_term(index):
        return jnp.dot(merged_of(index), q_full, precision=high)
    replica_ids = jnp.arange(REPLICAS, dtype=jnp.int32)
    p_sum = jnp.sum(lax.map(left_term, replica_ids), axis=0)
    gram = jnp.dot(p_sum.T, p_sum, precision=high)
    chol = jnp.linalg.cholesky(gram)
    p_basis = jax.scipy.linalg.solve_triangular(chol, p_sum.T, lower=True).T

    def right_term(index):
        return jnp.dot(merged_of(index).T, p_basis, precision=high)
    q_factor = jnp.sum(lax.map(right_term, replica_ids), axis=0) / REPLICAS

    def rebuild(index):
        return (merged_of(index) - jnp.dot(p_basis, q_factor.T, precision=high)).astype(jnp.bfloat16)
    residual = lax.map(rebuild, replica_ids)
    return (residual, p_basis, q_factor)
```

```python
import math

import jax
import jax.numpy as jnp
from jax import lax
from jax.experimental import pallas as pl
from jax.experimental.pallas import tpu as pltpu
from jax.sharding import PartitionSpec as P

F32 = jnp.float32
BF16 = jnp.bfloat16
VMEM = pl.BlockSpec(memory_space=pltpu.VMEM)
PARAMS = pltpu.CompilerParams(vmem_limit_bytes=32 * 1024 * 1024)
STREAM = pltpu.CompilerParams(vmem_limit_bytes=60 * 1024 * 1024)


def parts_of(x, n):
    out = []
    for _ in range(n):
        part = x.astype(BF16)
        out.append(part)
        x = x - part.astype(F32)
    return out


def dot(a, b, a_dim=1, b_dim=0):
    return lax.dot_general(
        a, b, (((a_dim,), (b_dim,)), ((), ())), preferred_element_type=F32
    )


def cost(flops, moved):
    return pl.CostEstimate(flops=flops, bytes_accessed=moved, transcendentals=0)


def y_kernel(q_ref, g_ref, out_ref, q_buf, g_buf, q_sem, g_sems):
    n, _, rows = out_ref.shape
    q_copy = pltpu.make_async_copy(q_ref, q_buf, q_sem)
    copies = [
        pltpu.make_async_copy(
            g_ref.at[pl.ds(s * rows, rows), :],
            g_buf.at[pl.ds(s * rows, rows), :],
            g_sems.at[s],
        )
        for s in range(n)
    ]
    q_copy.start()
    for copy in copies:
        copy.start()
    q_copy.wait()
    for s in range(n):
        copies[s].wait()
        out_ref[s] = dot(q_buf[...], g_buf[s * rows : (s + 1) * rows, :], 1, 1)


def y_chunks(q_t, grads, n):
    rank, cols = q_t.shape
    rows = grads.shape[0] // n
    hbm = pl.BlockSpec(memory_space=pltpu.HBM)
    return pl.pallas_call(
        y_kernel,
        in_specs=[hbm, hbm],
        out_specs=VMEM,
        out_shape=jax.ShapeDtypeStruct((n, rank, rows), F32),
        scratch_shapes=[
            pltpu.VMEM(q_t.shape, BF16),
            pltpu.VMEM(grads.shape, BF16),
            pltpu.SemaphoreType.DMA,
            pltpu.SemaphoreType.DMA((n,)),
        ],
        compiler_params=STREAM,
        cost_estimate=cost(2 * grads.size * rank * 8, grads.size * 2),
        name="y_chunks",
    )(q_t, grads)


def e_kernel(q_ref, e_ref, out_ref):
    out_ref[...] = dot(q_ref[...], e_ref[...], 1, 1)


def error_term(q_t, error):
    return pl.pallas_call(
        e_kernel,
        in_specs=[VMEM] * 2,
        out_specs=VMEM,
        out_shape=jax.ShapeDtypeStruct((q_t.shape[0], error.shape[0]), F32),
        compiler_params=PARAMS,
        cost_estimate=cost(2 * error.size * 32 * 8, error.size * 2),
        name="error_term",
    )(q_t, error)


def p_kernel(y_ref, acts_ref, e_ref, out_ref):
    n, rank, width = out_ref.shape
    y = y_ref[0]
    for s in range(1, n):
        y = y + y_ref[s]
    stack = jnp.concatenate(parts_of(y, 3), axis=0)
    p = dot(stack, acts_ref[...])
    p = (p[:rank] + e_ref[...]) + (p[rank : 2 * rank] + p[2 * rank :])
    for s in range(n):
        out_ref[s] = p[:, s * width : (s + 1) * width]


def p_chunks(y_all, acts, e_term):
    n, rank, _ = y_all.shape
    width = acts.shape[1] // n
    return pl.pallas_call(
        p_kernel,
        in_specs=[VMEM] * 3,
        out_specs=VMEM,
        out_shape=jax.ShapeDtypeStruct((n, rank, width), F32),
        compiler_params=PARAMS,
        cost_estimate=cost(2 * acts.size * rank * 8, acts.size * 2),
        name="p_chunks",
    )(y_all, acts, e_term)


def merged_kernel(a_ref, g_ref, e_ref, after_ref, hi_ref, lo_ref):
    del after_ref
    merged = dot(a_ref[...], g_ref[...], 0, 0) + e_ref[...].astype(F32)
    hi, lo = parts_of(merged, 2)
    hi_ref[...] = hi
    lo_ref[...] = lo


def merged_parts(acts_all, grads, error, after):
    tokens, width = acts_all.shape
    cols = grads.shape[1]
    block = 256
    shape = jax.ShapeDtypeStruct((width, cols), BF16)
    out = pl.BlockSpec((block, cols), lambda i: (i, 0))
    return pl.pallas_call(
        merged_kernel,
        grid=(width // block,),
        in_specs=[
            pl.BlockSpec((tokens, block), lambda i: (0, i)),
            pl.BlockSpec((tokens, cols), lambda i: (0, 0)),
            out,
            pl.BlockSpec(memory_space=pl.ANY),
        ],
        out_specs=[out, out],
        out_shape=[shape, shape],
        compiler_params=PARAMS,
        cost_estimate=cost(2 * tokens * width * cols, acts_all.size * 2 + grads.size * 2),
        name="merged_parts",
    )(acts_all, grads, error, after)


def q_kernel(p_ref, hi_ref, lo_ref, out_ref):
    n, rank, width = p_ref.shape
    pieces, rows, _ = out_ref.shape
    total = None
    for s in range(n):
        high, low = parts_of(p_ref[s], 2)
        span = slice(s * width, (s + 1) * width)
        both = dot(jnp.concatenate([high, low], axis=0), hi_ref[span, :])
        term = both[:rank] + (both[rank:] + dot(high, lo_ref[span, :]))
        total = term if total is None else total + term
    for k in range(pieces):
        out_ref[k] = total[k * rows : (k + 1) * rows, :]


def q_pieces(p_all, hi, lo, pieces):
    n, rank, width = p_all.shape
    cols = hi.shape[1]
    return pl.pallas_call(
        q_kernel,
        in_specs=[VMEM] * 3,
        out_specs=VMEM,
        out_shape=jax.ShapeDtypeStruct((pieces, rank // pieces, cols), F32),
        compiler_params=PARAMS,
        cost_estimate=cost(2 * hi.size * rank * 8, hi.size * 4),
        name="q_pieces",
    )(p_all, hi, lo)


def basis_kernel(p_ref, after_ref, inv_ref, basis_ref, stack_ref, full_ref):
    del after_ref
    n, rank, width = p_ref.shape
    for s in range(n):
        full_ref[:, s * width : (s + 1) * width] = p_ref[s]
    p = full_ref[...]
    gram = lax.dot_general(
        p,
        p,
        (((1,), (1,)), ((), ())),
        precision=lax.Precision.HIGHEST,
        preferred_element_type=F32,
    )
    row = lax.broadcasted_iota(jnp.int32, (rank, rank), 0)
    col = lax.broadcasted_iota(jnp.int32, (rank, rank), 1)
    eye = (row == col).astype(F32)
    work = jnp.concatenate([gram, eye], axis=1)
    below = lax.broadcasted_iota(jnp.int32, (rank, 1), 0)
    for j in range(rank - 1):
        pivot = work[j : j + 1, :]
        factor = jnp.where(below > j, work[:, j : j + 1] / pivot[:, j : j + 1], 0.0)
        work = work - factor * pivot
    upper = work[:, :rank]
    pivots = jnp.sum(jnp.where(row == col, upper, 0.0), axis=1, keepdims=True)
    inverse = work[:, rank:] / jnp.sqrt(pivots)
    inv_ref[...] = inverse
    basis = jnp.dot(
        inverse, p, precision=lax.Precision.HIGHEST, preferred_element_type=F32
    )
    basis_ref[...] = basis
    high = basis.astype(BF16).astype(F32)
    low = basis - high
    wide = jnp.concatenate([high, high, low, jnp.zeros_like(low)], axis=0)
    stack_ref[...] = wide.T.astype(BF16)


def basis_of(p_all, after):
    n, rank, width = p_all.shape
    size = n * width
    return pl.pallas_call(
        basis_kernel,
        in_specs=[VMEM, pl.BlockSpec(memory_space=pl.ANY)],
        out_specs=[VMEM] * 3,
        out_shape=[
            jax.ShapeDtypeStruct((rank, rank), F32),
            jax.ShapeDtypeStruct((rank, size), F32),
            jax.ShapeDtypeStruct((size, 4 * rank), BF16),
        ],
        scratch_shapes=[pltpu.VMEM((rank, size), F32)],
        compiler_params=PARAMS,
        cost_estimate=cost(4_000_000_000, 4_000_000),
        name="basis",
    )(p_all, after)


def residual_kernel(scale, q_ref, inv_ref, stack_ref, hi_ref, lo_ref, out_ref, factor_ref, raw, tall):
    @pl.when(pl.program_id(0) == 0)
    def _():
        pieces, rows, _ = q_ref.shape
        for k in range(pieces):
            raw[k * rows : (k + 1) * rows, :] = q_ref[k]
        factor = scale * jnp.dot(
            inv_ref[...],
            raw[...],
            precision=lax.Precision.HIGHEST,
            preferred_element_type=F32,
        )
        factor_ref[...] = factor
        high, low = parts_of(factor, 2)
        tall[...] = jnp.concatenate([high, low, high, jnp.zeros_like(low)], axis=0)

    merged = hi_ref[...].astype(F32) + lo_ref[...].astype(F32)
    out_ref[...] = (merged - dot(stack_ref[...], tall[...])).astype(BF16)


def residual_of(q_all, inverse, stack, hi, lo, replicas):
    rank = inverse.shape[0]
    height, cols = hi.shape
    block = 256
    part = pl.BlockSpec((block, cols), lambda i: (i, 0))
    whole = lambda shape: pl.BlockSpec(shape, lambda i: (0,) * len(shape))
    return pl.pallas_call(
        lambda *refs: residual_kernel(1.0 / replicas, *refs),
        grid=(height // block,),
        in_specs=[
            whole(q_all.shape),
            whole(inverse.shape),
            pl.BlockSpec((block, stack.shape[1]), lambda i: (i, 0)),
            part,
            part,
        ],
        out_specs=[part, whole((rank, cols))],
        out_shape=[
            jax.ShapeDtypeStruct((height, cols), BF16),
            jax.ShapeDtypeStruct((rank, cols), F32),
        ],
        scratch_shapes=[
            pltpu.VMEM((rank, cols), F32),
            pltpu.VMEM((4 * rank, cols), BF16),
        ],
        compiler_params=PARAMS,
        name="residual",
    )(q_all, inverse, stack, hi, lo)


def total_kernel(x_ref, out_ref):
    total = x_ref[0]
    for s in range(1, x_ref.shape[0]):
        total = total + x_ref[s]
    for s in range(out_ref.shape[0]):
        out_ref[s] = total


def total_for(x, n):
    return pl.pallas_call(
        total_kernel,
        in_specs=[VMEM],
        out_specs=VMEM,
        out_shape=jax.ShapeDtypeStruct((n,) + x.shape[1:], F32),
        compiler_params=PARAMS,
        cost_estimate=cost(x.size, 4 * x.size),
        name="total",
    )(x)


def per_device(acts, grads_out, error_buffer, prior_q):
    tensor = lax.axis_size("tensor")
    replicas = lax.axis_size("dp")
    side = math.isqrt(replicas)
    along_y = [[y * side + z for y in range(side)] for z in range(side)]
    along_z = [[y * side + z for z in range(side)] for y in range(side)]

    def over_tensor(x):
        return lax.all_to_all(x, "tensor", 0, 0)

    def over_y(x):
        return lax.all_to_all(x, "dp", 0, 0, axis_index_groups=along_y)

    def over_z(x):
        return lax.all_to_all(x, "dp", 0, 0, axis_index_groups=along_z)

    error = error_buffer[0]
    q_t = prior_q.T
    acts_all = lax.all_gather(acts, "tensor", axis=0, tiled=True)

    y_all = over_tensor(y_chunks(q_t, grads_out, tensor))
    p_terms = over_tensor(p_chunks(y_all, acts, error_term(q_t, error)))
    p_row = total_for(over_y(total_for(p_terms, side)), side)
    p_all = over_tensor(total_for(over_z(p_row), tensor))

    hi, lo = merged_parts(acts_all, grads_out, error, p_row)
    pieces = q_pieces(p_all, hi, lo, side)
    q_sum = total_for(over_z(total_for(over_y(pieces), side)), side)
    q_all = over_y(q_sum)
    inverse, basis, stack = basis_of(p_all, pieces)
    residual, factor = residual_of(q_all, inverse, stack, hi, lo, replicas)
    return (residual[None], basis.T, factor.T)


def solution(mesh):
    in_specs = (
        P(("dp", "tensor"), None),
        P("dp", "tensor"),
        P("dp", None, "tensor"),
        P("tensor", None),
    )
    out_specs = (P("dp", None, "tensor"), P(), P("tensor", None))
    return jax.shard_map(
        per_device, mesh=mesh, in_specs=in_specs, out_specs=out_specs, check_vma=False
    )
```

```python
import math

import jax
import jax.numpy as jnp
from jax import lax
from jax.experimental import pallas as pl
from jax.experimental.pallas import tpu as pltpu
from jax.sharding import PartitionSpec as P

F32 = jnp.float32
BF16 = jnp.bfloat16
LANES = 128
VMEM = pl.BlockSpec(memory_space=pltpu.VMEM)
PARAMS = pltpu.CompilerParams(vmem_limit_bytes=32 * 1024 * 1024)
STREAM = pltpu.CompilerParams(vmem_limit_bytes=60 * 1024 * 1024)


def parts_of(x, n):
    out = []
    for _ in range(n):
        part = x.astype(BF16)
        out.append(part)
        x = x - part.astype(F32)
    return out


def dot(a, b, a_dim=1, b_dim=0):
    return lax.dot_general(
        a, b, (((a_dim,), (b_dim,)), ((), ())), preferred_element_type=F32
    )


def cost(flops, moved):
    return pl.CostEstimate(flops=flops, bytes_accessed=moved, transcendentals=0)


def y_kernel(q_ref, g_ref, out_ref, q_buf, g_buf, q_sem, g_sems):
    n, _, rows = out_ref.shape
    q_copy = pltpu.make_async_copy(q_ref, q_buf, q_sem)
    copies = [
        pltpu.make_async_copy(
            g_ref.at[pl.ds(s * rows, rows), :],
            g_buf.at[pl.ds(s * rows, rows), :],
            g_sems.at[s],
        )
        for s in range(n)
    ]
    q_copy.start()
    for copy in copies:
        copy.start()
    q_copy.wait()
    for s in range(n):
        copies[s].wait()
        out_ref[s] = dot(q_buf[...], g_buf[s * rows : (s + 1) * rows, :], 1, 1)


def y_chunks(q_t, grads, n):
    rank, cols = q_t.shape
    rows = grads.shape[0] // n
    hbm = pl.BlockSpec(memory_space=pltpu.HBM)
    return pl.pallas_call(
        y_kernel,
        in_specs=[hbm, hbm],
        out_specs=VMEM,
        out_shape=jax.ShapeDtypeStruct((n, rank, rows), F32),
        scratch_shapes=[
            pltpu.VMEM(q_t.shape, BF16),
            pltpu.VMEM(grads.shape, BF16),
            pltpu.SemaphoreType.DMA,
            pltpu.SemaphoreType.DMA((n,)),
        ],
        compiler_params=STREAM,
        cost_estimate=cost(2 * grads.size * rank * 8, grads.size * 2),
        name="y_chunks",
    )(q_t, grads)


def e_kernel(q_ref, e_ref, out_ref):
    out_ref[...] = dot(q_ref[...], e_ref[...], 1, 1)


def error_term(q_t, error):
    return pl.pallas_call(
        e_kernel,
        in_specs=[VMEM] * 2,
        out_specs=VMEM,
        out_shape=jax.ShapeDtypeStruct((q_t.shape[0], error.shape[0]), F32),
        compiler_params=PARAMS,
        cost_estimate=cost(2 * error.size * 32 * 8, error.size * 2),
        name="error_term",
    )(q_t, error)


def write_pieces(out_ref, x):
    pieces, rows, _ = out_ref.shape
    across = x.shape[1] // LANES
    for k in range(pieces):
        r, c = k // across, k % across
        out_ref[k] = x[r * rows : (r + 1) * rows, c * LANES : (c + 1) * LANES]


def read_pieces(in_ref, full_ref):
    pieces, rows, _ = in_ref.shape
    across = full_ref.shape[1] // LANES
    for k in range(pieces):
        r, c = k // across, k % across
        full_ref[r * rows : (r + 1) * rows, c * LANES : (c + 1) * LANES] = in_ref[k]


def p_kernel(y_ref, acts_ref, e_ref, out_ref):
    n, rank, _ = y_ref.shape
    y = y_ref[0]
    for s in range(1, n):
        y = y + y_ref[s]
    stack = jnp.concatenate(parts_of(y, 3), axis=0)
    p = dot(stack, acts_ref[...])
    write_pieces(
        out_ref, (p[:rank] + e_ref[...]) + (p[rank : 2 * rank] + p[2 * rank :])
    )


def p_pieces(y_all, acts, e_term, pieces):
    rows = e_term.size // (pieces * LANES)
    return pl.pallas_call(
        p_kernel,
        in_specs=[VMEM] * 3,
        out_specs=VMEM,
        out_shape=jax.ShapeDtypeStruct((pieces, rows, LANES), F32),
        compiler_params=PARAMS,
        cost_estimate=cost(2 * acts.size * 256, acts.size * 2),
        name="p_pieces",
    )(y_all, acts, e_term)


def merged_kernel(a_ref, g_ref, e_ref, after_ref, hi_ref, lo_ref):
    del after_ref
    merged = dot(a_ref[...], g_ref[...], 0, 0) + e_ref[...].astype(F32)
    hi, lo = parts_of(merged, 2)
    hi_ref[...] = hi
    lo_ref[...] = lo


def merged_parts(acts_all, grads, error, after):
    tokens, width = acts_all.shape
    cols = grads.shape[1]
    block = 256
    shape = jax.ShapeDtypeStruct((width, cols), BF16)
    out = pl.BlockSpec((block, cols), lambda i: (i, 0))
    return pl.pallas_call(
        merged_kernel,
        grid=(width // block,),
        in_specs=[
            pl.BlockSpec((tokens, block), lambda i: (0, i)),
            pl.BlockSpec((tokens, cols), lambda i: (0, 0)),
            out,
            pl.BlockSpec(memory_space=pl.ANY),
        ],
        out_specs=[out, out],
        out_shape=[shape, shape],
        compiler_params=PARAMS,
        cost_estimate=cost(2 * tokens * width * cols, acts_all.size * 2 + grads.size * 2),
        name="merged_parts",
    )(acts_all, grads, error, after)


def q_kernel(p_ref, hi_ref, lo_ref, out_ref, full_ref):
    read_pieces(p_ref, full_ref)
    rank = full_ref.shape[0]
    high, low = parts_of(full_ref[...], 2)
    both = dot(jnp.concatenate([high, low], axis=0), hi_ref[...])
    write_pieces(out_ref, both[:rank] + (both[rank:] + dot(high, lo_ref[...])))


def q_pieces(p_all, hi, lo, pieces):
    height, cols = hi.shape
    rank = p_all.size // height
    rows = rank * cols // (pieces * LANES)
    return pl.pallas_call(
        q_kernel,
        in_specs=[VMEM] * 3,
        out_specs=VMEM,
        out_shape=jax.ShapeDtypeStruct((pieces, rows, LANES), F32),
        scratch_shapes=[pltpu.VMEM((rank, height), F32)],
        compiler_params=PARAMS,
        cost_estimate=cost(2 * hi.size * rank * 8, hi.size * 4),
        name="q_pieces",
    )(p_all, hi, lo)


def basis_kernel(p_ref, after_ref, inv_ref, basis_ref, stack_ref, full_ref):
    del after_ref
    read_pieces(p_ref, full_ref)
    p = full_ref[...]
    rank = p.shape[0]
    gram = lax.dot_general(
        p,
        p,
        (((1,), (1,)), ((), ())),
        precision=lax.Precision.HIGHEST,
        preferred_element_type=F32,
    )
    row = lax.broadcasted_iota(jnp.int32, (rank, rank), 0)
    col = lax.broadcasted_iota(jnp.int32, (rank, rank), 1)
    eye = (row == col).astype(F32)
    work = jnp.concatenate([gram, eye], axis=1)
    below = lax.broadcasted_iota(jnp.int32, (rank, 1), 0)
    for j in range(rank - 1):
        pivot = work[j : j + 1, :]
        factor = jnp.where(below > j, work[:, j : j + 1] / pivot[:, j : j + 1], 0.0)
        work = work - factor * pivot
    upper = work[:, :rank]
    pivots = jnp.sum(jnp.where(row == col, upper, 0.0), axis=1, keepdims=True)
    inverse = work[:, rank:] / jnp.sqrt(pivots)
    inv_ref[...] = inverse
    basis = jnp.dot(
        inverse, p, precision=lax.Precision.HIGHEST, preferred_element_type=F32
    )
    basis_ref[...] = basis
    high = basis.astype(BF16).astype(F32)
    low = basis - high
    wide = jnp.concatenate([high, high, low, jnp.zeros_like(low)], axis=0)
    stack_ref[...] = wide.T.astype(BF16)


def basis_of(p_all, after, rank):
    size = p_all.size // rank
    return pl.pallas_call(
        basis_kernel,
        in_specs=[VMEM, pl.BlockSpec(memory_space=pl.ANY)],
        out_specs=[VMEM] * 3,
        out_shape=[
            jax.ShapeDtypeStruct((rank, rank), F32),
            jax.ShapeDtypeStruct((rank, size), F32),
            jax.ShapeDtypeStruct((size, 4 * rank), BF16),
        ],
        scratch_shapes=[pltpu.VMEM((rank, size), F32)],
        compiler_params=PARAMS,
        cost_estimate=cost(4_000_000_000, 4_000_000),
        name="basis",
    )(p_all, after)


def residual_kernel(scale, q_ref, inv_ref, stack_ref, hi_ref, lo_ref, out_ref, factor_ref, raw, tall):
    @pl.when(pl.program_id(0) == 0)
    def _():
        read_pieces(q_ref, raw)
        factor = scale * jnp.dot(
            inv_ref[...],
            raw[...],
            precision=lax.Precision.HIGHEST,
            preferred_element_type=F32,
        )
        factor_ref[...] = factor
        high, low = parts_of(factor, 2)
        tall[...] = jnp.concatenate([high, low, high, jnp.zeros_like(low)], axis=0)

    merged = hi_ref[...].astype(F32) + lo_ref[...].astype(F32)
    out_ref[...] = (merged - dot(stack_ref[...], tall[...])).astype(BF16)


def residual_of(q_all, inverse, stack, hi, lo, replicas):
    rank = inverse.shape[0]
    height, cols = hi.shape
    block = 256
    part = pl.BlockSpec((block, cols), lambda i: (i, 0))
    whole = lambda shape: pl.BlockSpec(shape, lambda i: (0,) * len(shape))
    return pl.pallas_call(
        lambda *refs: residual_kernel(1.0 / replicas, *refs),
        grid=(height // block,),
        in_specs=[
            whole(q_all.shape),
            whole(inverse.shape),
            pl.BlockSpec((block, stack.shape[1]), lambda i: (i, 0)),
            part,
            part,
        ],
        out_specs=[part, whole((rank, cols))],
        out_shape=[
            jax.ShapeDtypeStruct((height, cols), BF16),
            jax.ShapeDtypeStruct((rank, cols), F32),
        ],
        scratch_shapes=[
            pltpu.VMEM((rank, cols), F32),
            pltpu.VMEM((4 * rank, cols), BF16),
        ],
        compiler_params=PARAMS,
        name="residual",
    )(q_all, inverse, stack, hi, lo)


def total_kernel(x_ref, out_ref):
    total = x_ref[0]
    for s in range(1, x_ref.shape[0]):
        total = total + x_ref[s]
    out_ref[...] = total


def total_of(x):
    return pl.pallas_call(
        total_kernel,
        in_specs=[VMEM],
        out_specs=VMEM,
        out_shape=jax.ShapeDtypeStruct(x.shape[1:], F32),
        compiler_params=PARAMS,
        cost_estimate=cost(x.size, 4 * x.size),
        name="total",
    )(x)


def exchange(x, axis, groups):
    return lax.all_to_all(x, axis, 0, 0, axis_index_groups=groups)


def to_all(x, axis, groups):
    n = len(groups[0])
    return exchange(jnp.broadcast_to(x[None], (n,) + x.shape), axis, groups)


def add_partner(x, distance):
    pairs = [(i, i ^ distance) for i in range(lax.axis_size("dp"))]
    return x + lax.ppermute(x, "dp", pairs)


def per_device(acts, grads_out, error_buffer, prior_q):
    tensor = lax.axis_size("tensor")
    replicas = lax.axis_size("dp")
    side = math.isqrt(replicas)
    half = side // 2
    along_y = [[y * side + z for y in range(side)] for z in range(side)]
    for_p = [
        [(y * side + h * half + z) * tensor + t for h in range(2) for t in range(tensor)]
        for y in range(side)
        for z in range(half)
    ]
    for_q = [
        [y * side + 2 * h + z for y in range(side) for h in range(half)]
        for z in range(2)
    ]
    both = ("dp", "tensor")

    error = error_buffer[0]
    q_t = prior_q.T
    rank = q_t.shape[0]
    acts_all = lax.all_gather(acts, "tensor", axis=0, tiled=True)

    y_all = lax.all_to_all(y_chunks(q_t, grads_out, tensor), "tensor", 0, 0)
    p_mine = p_pieces(y_all, acts, error_term(q_t, error), 2 * tensor)
    p_mine = total_of(exchange(p_mine, both, for_p))
    p_mine = lax.psum(p_mine, "dp", axis_index_groups=along_y)
    after = p_mine
    distance = 1
    while distance < half:
        p_mine = add_partner(p_mine, distance)
        distance *= 2
    p_all = to_all(p_mine, both, for_p)

    hi, lo = merged_parts(acts_all, grads_out, error, after)
    pieces = q_pieces(p_all, hi, lo, side * half)
    q_mine = add_partner(total_of(exchange(pieces, "dp", for_q)), 1)
    q_all = to_all(q_mine, "dp", for_q)
    inverse, basis, stack = basis_of(p_all, q_mine, rank)
    residual, factor = residual_of(q_all, inverse, stack, hi, lo, replicas)
    return (residual[None], basis.T, factor.T)


def solution(mesh):
    in_specs = (
        P(("dp", "tensor"), None),
        P("dp", "tensor"),
        P("dp", None, "tensor"),
        P("tensor", None),
    )
    out_specs = (P("dp", None, "tensor"), P(), P("tensor", None))
    return jax.shard_map(
        per_device, mesh=mesh, in_specs=in_specs, out_specs=out_specs, check_vma=False
    )
```

```python
import math

import jax
import jax.numpy as jnp
from jax import lax
from jax.experimental import pallas as pl
from jax.experimental.pallas import tpu as pltpu
from jax.sharding import PartitionSpec as P

F32 = jnp.float32
BF16 = jnp.bfloat16
LANES = 128
VMEM = pl.BlockSpec(memory_space=pltpu.VMEM)
HBM = pl.BlockSpec(memory_space=pltpu.HBM)
ANY = pl.BlockSpec(memory_space=pl.ANY)
PARAMS = pltpu.CompilerParams(vmem_limit_bytes=32 * 1024 * 1024)
STREAM = pltpu.CompilerParams(vmem_limit_bytes=60 * 1024 * 1024)


def parts_of(x, n):
    out = []
    for _ in range(n):
        part = x.astype(BF16)
        out.append(part)
        x = x - part.astype(F32)
    return out


def dot(a, b, a_dim=1, b_dim=0):
    return lax.dot_general(
        a, b, (((a_dim,), (b_dim,)), ((), ())), preferred_element_type=F32
    )


def cost(flops, moved):
    return pl.CostEstimate(flops=flops, bytes_accessed=moved, transcendentals=0)


def y_kernel(q_ref, g_ref, out_ref, q_buf, g_buf, y_buf, q_sem, g_sems, y_sems):
    n, _, rows = out_ref.shape
    q_copy = pltpu.make_async_copy(q_ref, q_buf, q_sem)
    q_copy.start()
    loads, stores = [], []
    for s in range(n):
        span = pl.ds(s * rows, rows)
        loads.append(
            pltpu.make_async_copy(g_ref.at[span, :], g_buf.at[span, :], g_sems.at[s])
        )
        stores.append(pltpu.make_async_copy(y_buf.at[s], out_ref.at[s], y_sems.at[s]))
        loads[s].start()
    q_copy.wait()
    for s in range(n):
        loads[s].wait()
        y_buf[s] = dot(q_buf[...], g_buf[s * rows : (s + 1) * rows, :], 1, 1)
        stores[s].start()
    for s in range(n):
        stores[s].wait()


def y_chunks(q_t, grads, n):
    rank, cols = q_t.shape
    rows = grads.shape[0] // n
    return pl.pallas_call(
        y_kernel,
        in_specs=[HBM, HBM],
        out_specs=HBM,
        out_shape=jax.ShapeDtypeStruct((n, rank, rows), F32),
        scratch_shapes=[
            pltpu.VMEM(q_t.shape, BF16),
            pltpu.VMEM(grads.shape, BF16),
            pltpu.VMEM((n, rank, rows), F32),
            pltpu.SemaphoreType.DMA,
            pltpu.SemaphoreType.DMA((n,)),
            pltpu.SemaphoreType.DMA((n,)),
        ],
        compiler_params=STREAM,
        cost_estimate=cost(2 * grads.size * rank * 8, grads.size * 2),
        name="y_chunks",
    )(q_t, grads)


def e_kernel(q_ref, e_ref, out_ref):
    out_ref[...] = dot(q_ref[...], e_ref[...], 1, 1)


def error_term(q_t, error):
    return pl.pallas_call(
        e_kernel,
        in_specs=[VMEM] * 2,
        out_specs=VMEM,
        out_shape=jax.ShapeDtypeStruct((q_t.shape[0], error.shape[0]), F32),
        compiler_params=PARAMS,
        cost_estimate=cost(2 * error.size * 32 * 8, error.size * 2),
        name="error_term",
    )(q_t, error)


def p_kernel(y_ref, acts_ref, e_ref, out_ref):
    n, rank, width = out_ref.shape
    y = y_ref[0]
    for s in range(1, n):
        y = y + y_ref[s]
    stack = jnp.concatenate(parts_of(y, 3), axis=0)
    p = dot(stack, acts_ref[...])
    p = (p[:rank] + e_ref[...]) + (p[rank : 2 * rank] + p[2 * rank :])
    for s in range(n):
        out_ref[s] = p[:, s * width : (s + 1) * width]


def p_chunks(y_all, acts, e_term):
    n, rank, _ = y_all.shape
    width = acts.shape[1] // n
    return pl.pallas_call(
        p_kernel,
        in_specs=[VMEM] * 3,
        out_specs=VMEM,
        out_shape=jax.ShapeDtypeStruct((n, rank, width), F32),
        compiler_params=PARAMS,
        cost_estimate=cost(2 * acts.size * rank * 8, acts.size * 2),
        name="p_chunks",
    )(y_all, acts, e_term)


def merged_kernel(a_ref, g_ref, e_ref, after_ref, hi_ref, lo_ref):
    del after_ref
    merged = dot(a_ref[...], g_ref[...], 0, 0) + e_ref[...].astype(F32)
    hi, lo = parts_of(merged, 2)
    hi_ref[...] = hi
    lo_ref[...] = lo


def merged_parts(acts_all, grads, error, after):
    tokens, width = acts_all.shape
    cols = grads.shape[1]
    block = 256
    shape = jax.ShapeDtypeStruct((width, cols), BF16)
    out = pl.BlockSpec((block, cols), lambda i: (i, 0))
    return pl.pallas_call(
        merged_kernel,
        grid=(width // block,),
        in_specs=[
            pl.BlockSpec((tokens, block), lambda i: (0, i)),
            pl.BlockSpec((tokens, cols), lambda i: (0, 0)),
            out,
            ANY,
        ],
        out_specs=[out, out],
        out_shape=[shape, shape],
        compiler_params=STREAM,
        cost_estimate=cost(2 * tokens * width * cols, acts_all.size * 2 + grads.size * 2),
        name="merged_parts",
    )(acts_all, grads, error, after)


def q_kernel(p_ref, hi_ref, lo_ref, out_ref):
    n, rank, width = p_ref.shape
    pieces, rows, _ = out_ref.shape
    total = None
    for s in range(n):
        high, low = parts_of(p_ref[s], 2)
        span = slice(s * width, (s + 1) * width)
        both = dot(jnp.concatenate([high, low], axis=0), hi_ref[span, :])
        term = both[:rank] + (both[rank:] + dot(high, lo_ref[span, :]))
        total = term if total is None else total + term
    across = total.shape[1] // LANES
    for k in range(pieces):
        r, c = k // across, k % across
        out_ref[k] = total[r * rows : (r + 1) * rows, c * LANES : (c + 1) * LANES]


def q_pieces(p_all, hi, lo, pieces):
    n, rank, width = p_all.shape
    cols = hi.shape[1]
    rows = rank * cols // (pieces * LANES)
    return pl.pallas_call(
        q_kernel,
        in_specs=[VMEM] * 3,
        out_specs=VMEM,
        out_shape=jax.ShapeDtypeStruct((pieces, rows, LANES), F32),
        compiler_params=PARAMS,
        cost_estimate=cost(2 * hi.size * rank * 8, hi.size * 4),
        name="q_pieces",
    )(p_all, hi, lo)


def basis_kernel(p_ref, after_ref, inv_ref, basis_ref, stack_ref, full_ref):
    del after_ref
    n, rank, width = p_ref.shape
    for s in range(n):
        full_ref[:, s * width : (s + 1) * width] = p_ref[s]
    p = full_ref[...]
    gram = lax.dot_general(
        p,
        p,
        (((1,), (1,)), ((), ())),
        precision=lax.Precision.HIGHEST,
        preferred_element_type=F32,
    )
    row = lax.broadcasted_iota(jnp.int32, (rank, rank), 0)
    col = lax.broadcasted_iota(jnp.int32, (rank, rank), 1)
    eye = (row == col).astype(F32)
    work = jnp.concatenate([gram, eye], axis=1)
    below = lax.broadcasted_iota(jnp.int32, (rank, 1), 0)
    for j in range(rank - 1):
        pivot = work[j : j + 1, :]
        factor = jnp.where(below > j, work[:, j : j + 1] / pivot[:, j : j + 1], 0.0)
        work = work - factor * pivot
    upper = work[:, :rank]
    pivots = jnp.sum(jnp.where(row == col, upper, 0.0), axis=1, keepdims=True)
    inverse = work[:, rank:] / jnp.sqrt(pivots)
    inv_ref[...] = inverse
    basis = jnp.dot(
        inverse, p, precision=lax.Precision.HIGHEST, preferred_element_type=F32
    )
    basis_ref[...] = basis
    high = basis.astype(BF16).astype(F32)
    low = basis - high
    wide = jnp.concatenate([high, high, low, jnp.zeros_like(low)], axis=0)
    stack_ref[...] = wide.T.astype(BF16)


def basis_of(p_all, after):
    n, rank, width = p_all.shape
    size = n * width
    return pl.pallas_call(
        basis_kernel,
        in_specs=[VMEM, ANY],
        out_specs=[VMEM] * 3,
        out_shape=[
            jax.ShapeDtypeStruct((rank, rank), F32),
            jax.ShapeDtypeStruct((rank, size), F32),
            jax.ShapeDtypeStruct((size, 4 * rank), BF16),
        ],
        scratch_shapes=[pltpu.VMEM((rank, size), F32)],
        compiler_params=PARAMS,
        cost_estimate=cost(4_000_000_000, 4_000_000),
        name="basis",
    )(p_all, after)


def residual_kernel(scale, q_ref, inv_ref, stack_ref, hi_ref, lo_ref, out_ref, factor_ref, raw, factor, out_buf, sems, factor_sem):
    pieces, rows, _ = q_ref.shape
    across = raw.shape[1] // LANES
    for k in range(pieces):
        r, c = k // across, k % across
        raw[r * rows : (r + 1) * rows, c * LANES : (c + 1) * LANES] = q_ref[k]
    factor[...] = scale * jnp.dot(
        inv_ref[...],
        raw[...],
        precision=lax.Precision.HIGHEST,
        preferred_element_type=F32,
    )
    copies = [pltpu.make_async_copy(factor, factor_ref, factor_sem)]
    copies[0].start()
    high, low = parts_of(factor[...], 2)
    tall = jnp.concatenate([high, low, high, jnp.zeros_like(low)], axis=0)
    blocks = sems.shape[0]
    block = out_ref.shape[0] // blocks
    for i in range(blocks):
        span = pl.ds(i * block, block)
        merged = hi_ref[span, :].astype(F32) + lo_ref[span, :].astype(F32)
        out_buf[span, :] = (merged - dot(stack_ref[span, :], tall)).astype(BF16)
        copies.append(
            pltpu.make_async_copy(out_buf.at[span, :], out_ref.at[span, :], sems.at[i])
        )
        copies[-1].start()
    for copy in copies:
        copy.wait()


def residual_of(q_all, inverse, stack, hi, lo, replicas):
    rank = inverse.shape[0]
    cols = hi.shape[1]
    return pl.pallas_call(
        lambda *refs: residual_kernel(1.0 / replicas, *refs),
        in_specs=[VMEM] * 5,
        out_specs=[HBM, HBM],
        out_shape=[
            jax.ShapeDtypeStruct(hi.shape, BF16),
            jax.ShapeDtypeStruct((rank, cols), F32),
        ],
        scratch_shapes=[
            pltpu.VMEM((rank, cols), F32),
            pltpu.VMEM((rank, cols), F32),
            pltpu.VMEM(hi.shape, BF16),
            pltpu.SemaphoreType.DMA((8,)),
            pltpu.SemaphoreType.DMA,
        ],
        compiler_params=PARAMS,
        name="residual",
    )(q_all, inverse, stack, hi, lo)


def total_kernel(x_ref, *refs):
    out_ref = refs[-1]
    total = x_ref[0]
    for s in range(1, x_ref.shape[0]):
        total = total + x_ref[s]
    for s in range(out_ref.shape[0]):
        out_ref[s] = total


def total_for(x, n, *after):
    return pl.pallas_call(
        total_kernel,
        in_specs=[VMEM] + [ANY] * len(after),
        out_specs=VMEM,
        out_shape=jax.ShapeDtypeStruct((n,) + x.shape[1:], F32),
        compiler_params=PARAMS,
        cost_estimate=cost(x.size, 4 * x.size),
        name="total",
    )(x, *after)


def per_device(acts, grads_out, error_buffer, prior_q):
    tensor = lax.axis_size("tensor")
    replicas = lax.axis_size("dp")
    side = math.isqrt(replicas)
    along_y = [[y * side + z for y in range(side)] for z in range(side)]
    along_z = [[y * side + z for z in range(side)] for y in range(side)]

    def over_tensor(x):
        return lax.all_to_all(x, "tensor", 0, 0)

    def over_y(x):
        return lax.all_to_all(x, "dp", 0, 0, axis_index_groups=along_y)

    def over_z(x):
        return lax.all_to_all(x, "dp", 0, 0, axis_index_groups=along_z)

    def over_replicas(x):
        return lax.all_to_all(x, "dp", 0, 0)

    error = error_buffer[0]
    q_t = prior_q.T
    acts_all = lax.all_gather(acts, "tensor", axis=0, tiled=True)

    y_all = over_tensor(y_chunks(q_t, grads_out, tensor))
    p_terms = over_tensor(p_chunks(y_all, acts, error_term(q_t, error)))
    p_row = total_for(over_y(total_for(p_terms, side)), side)
    hi, lo = merged_parts(acts_all, grads_out, error, p_row)
    p_all = over_tensor(total_for(over_z(p_row), tensor, hi))

    pieces = q_pieces(p_all, hi, lo, replicas)
    q_sum = total_for(over_replicas(pieces), replicas)
    q_all = over_replicas(q_sum)
    inverse, basis, stack = basis_of(p_all, q_sum)
    residual, factor = residual_of(q_all, inverse, stack, hi, lo, replicas)
    return (residual[None], basis.T, factor.T)


def solution(mesh):
    in_specs = (
        P(("dp", "tensor"), None),
        P("dp", "tensor"),
        P("dp", None, "tensor"),
        P("tensor", None),
    )
    out_specs = (P("dp", None, "tensor"), P(), P("tensor", None))
    return jax.shard_map(
        per_device, mesh=mesh, in_specs=in_specs, out_specs=out_specs, check_vma=False
    )
```

```python
import math

import jax
import jax.numpy as jnp
from jax import lax
from jax.experimental import pallas as pl
from jax.experimental.pallas import tpu as pltpu
from jax.sharding import PartitionSpec as P

F32 = jnp.float32
BF16 = jnp.bfloat16
VMEM = pl.BlockSpec(memory_space=pltpu.VMEM)
HBM = pl.BlockSpec(memory_space=pltpu.HBM)
ANY = pl.BlockSpec(memory_space=pl.ANY)
PARAMS = pltpu.CompilerParams(vmem_limit_bytes=32 * 1024 * 1024)
STREAM = pltpu.CompilerParams(vmem_limit_bytes=60 * 1024 * 1024)


def parts_of(x, n):
    out = []
    for _ in range(n):
        part = x.astype(BF16)
        out.append(part)
        x = x - part.astype(F32)
    return out


def dot(a, b, a_dim=1, b_dim=0):
    return lax.dot_general(
        a, b, (((a_dim,), (b_dim,)), ((), ())), preferred_element_type=F32
    )


def cost(flops, moved):
    return pl.CostEstimate(flops=flops, bytes_accessed=moved, transcendentals=0)


def y_kernel(q_ref, g_ref, out_ref, q_buf, g_buf, y_buf, q_sem, g_sems, y_sems):
    n, _, rows = out_ref.shape
    q_copy = pltpu.make_async_copy(q_ref, q_buf, q_sem)
    q_copy.start()
    loads, stores = [], []
    for s in range(n):
        span = pl.ds(s * rows, rows)
        loads.append(
            pltpu.make_async_copy(g_ref.at[span, :], g_buf.at[span, :], g_sems.at[s])
        )
        stores.append(pltpu.make_async_copy(y_buf.at[s], out_ref.at[s], y_sems.at[s]))
        loads[s].start()
    q_copy.wait()
    for s in range(n):
        loads[s].wait()
        y_buf[s] = dot(q_buf[...], g_buf[s * rows : (s + 1) * rows, :], 1, 1)
        stores[s].start()
    for s in range(n):
        stores[s].wait()


def y_chunks(q_t, grads, n):
    rank, cols = q_t.shape
    rows = grads.shape[0] // n
    return pl.pallas_call(
        y_kernel,
        in_specs=[HBM, HBM],
        out_specs=HBM,
        out_shape=jax.ShapeDtypeStruct((n, rank, rows), F32),
        scratch_shapes=[
            pltpu.VMEM(q_t.shape, BF16),
            pltpu.VMEM(grads.shape, BF16),
            pltpu.VMEM((n, rank, rows), F32),
            pltpu.SemaphoreType.DMA,
            pltpu.SemaphoreType.DMA((n,)),
            pltpu.SemaphoreType.DMA((n,)),
        ],
        compiler_params=STREAM,
        cost_estimate=cost(2 * grads.size * rank * 8, grads.size * 2),
        name="y_chunks",
    )(q_t, grads)


def e_kernel(q_ref, e_ref, out_ref):
    out_ref[...] = dot(q_ref[...], e_ref[...], 1, 1)


def error_term(q_t, error):
    return pl.pallas_call(
        e_kernel,
        in_specs=[VMEM] * 2,
        out_specs=VMEM,
        out_shape=jax.ShapeDtypeStruct((q_t.shape[0], error.shape[0]), F32),
        compiler_params=PARAMS,
        cost_estimate=cost(2 * error.size * 32 * 8, error.size * 2),
        name="error_term",
    )(q_t, error)


def p_kernel(y_ref, acts_ref, e_ref, out_ref):
    n, rank, width = out_ref.shape
    y = y_ref[0]
    for s in range(1, n):
        y = y + y_ref[s]
    stack = jnp.concatenate(parts_of(y, 3), axis=0)
    p = dot(stack, acts_ref[...])
    p = (p[:rank] + e_ref[...]) + (p[rank : 2 * rank] + p[2 * rank :])
    for s in range(n):
        out_ref[s] = p[:, s * width : (s + 1) * width]


def p_chunks(y_all, acts, e_term):
    n, rank, _ = y_all.shape
    width = acts.shape[1] // n
    return pl.pallas_call(
        p_kernel,
        in_specs=[VMEM] * 3,
        out_specs=VMEM,
        out_shape=jax.ShapeDtypeStruct((n, rank, width), F32),
        compiler_params=PARAMS,
        cost_estimate=cost(2 * acts.size * rank * 8, acts.size * 2),
        name="p_chunks",
    )(y_all, acts, e_term)


def merged_kernel(a_ref, g_ref, e_ref, after_ref, hi_ref, lo_ref):
    del after_ref
    block = 256

    @pl.loop(0, a_ref.shape[1] // block)
    def _(i):
        span = pl.ds(pl.multiple_of(i * block, block), block)
        merged = dot(a_ref[:, span], g_ref[...], 0, 0) + e_ref[span, :].astype(F32)
        hi, lo = parts_of(merged, 2)
        hi_ref[span, :] = hi
        lo_ref[span, :] = lo


def merged_parts(acts_all, grads, error, after):
    tokens, width = acts_all.shape
    cols = grads.shape[1]
    shape = jax.ShapeDtypeStruct((width, cols), BF16)
    return pl.pallas_call(
        merged_kernel,
        in_specs=[VMEM, VMEM, VMEM, ANY],
        out_specs=[VMEM, VMEM],
        out_shape=[shape, shape],
        compiler_params=PARAMS,
        cost_estimate=cost(2 * tokens * width * cols, acts_all.size * 2 + grads.size * 2),
        name="merged_parts",
    )(acts_all, grads, error, after)


def q_kernel(p_ref, hi_ref, lo_ref, out_ref):
    n, rank, width = p_ref.shape
    pieces, rows, _ = out_ref.shape
    total = None
    for s in range(n):
        high, low = parts_of(p_ref[s], 2)
        span = slice(s * width, (s + 1) * width)
        both = dot(jnp.concatenate([high, low], axis=0), hi_ref[span, :])
        term = both[:rank] + (both[rank:] + dot(high, lo_ref[span, :]))
        total = term if total is None else total + term
    for k in range(pieces):
        out_ref[k] = total[k * rows : (k + 1) * rows, :]


def q_pieces(p_all, hi, lo, pieces):
    n, rank, width = p_all.shape
    cols = hi.shape[1]
    return pl.pallas_call(
        q_kernel,
        in_specs=[VMEM] * 3,
        out_specs=VMEM,
        out_shape=jax.ShapeDtypeStruct((pieces, rank // pieces, cols), F32),
        compiler_params=PARAMS,
        cost_estimate=cost(2 * hi.size * rank * 8, hi.size * 4),
        name="q_pieces",
    )(p_all, hi, lo)


def basis_kernel(p_ref, after_ref, inv_ref, basis_ref, stack_ref, full_ref):
    del after_ref
    n, rank, width = p_ref.shape
    for s in range(n):
        full_ref[:, s * width : (s + 1) * width] = p_ref[s]
    p = full_ref[...]
    gram = lax.dot_general(
        p,
        p,
        (((1,), (1,)), ((), ())),
        precision=lax.Precision.HIGHEST,
        preferred_element_type=F32,
    )
    row = lax.broadcasted_iota(jnp.int32, (rank, rank), 0)
    col = lax.broadcasted_iota(jnp.int32, (rank, rank), 1)
    eye = (row == col).astype(F32)
    work = jnp.concatenate([gram, eye], axis=1)
    below = lax.broadcasted_iota(jnp.int32, (rank, 1), 0)
    for j in range(rank - 1):
        pivot = work[j : j + 1, :]
        factor = jnp.where(below > j, work[:, j : j + 1] / pivot[:, j : j + 1], 0.0)
        work = work - factor * pivot
    upper = work[:, :rank]
    pivots = jnp.sum(jnp.where(row == col, upper, 0.0), axis=1, keepdims=True)
    inverse = work[:, rank:] / jnp.sqrt(pivots)
    inv_ref[...] = inverse
    basis = jnp.dot(
        inverse, p, precision=lax.Precision.HIGHEST, preferred_element_type=F32
    )
    basis_ref[...] = basis
    high = basis.astype(BF16).astype(F32)
    low = basis - high
    wide = jnp.concatenate([high, high, low, jnp.zeros_like(low)], axis=0)
    stack_ref[...] = wide.T.astype(BF16)


def basis_of(p_all, after):
    n, rank, width = p_all.shape
    size = n * width
    return pl.pallas_call(
        basis_kernel,
        in_specs=[VMEM, ANY],
        out_specs=[VMEM] * 3,
        out_shape=[
            jax.ShapeDtypeStruct((rank, rank), F32),
            jax.ShapeDtypeStruct((rank, size), F32),
            jax.ShapeDtypeStruct((size, 4 * rank), BF16),
        ],
        scratch_shapes=[pltpu.VMEM((rank, size), F32)],
        compiler_params=PARAMS,
        cost_estimate=cost(4_000_000_000, 4_000_000),
        name="basis",
    )(p_all, after)


def residual_kernel(scale, q_ref, inv_ref, stack_ref, hi_ref, lo_ref, out_ref, factor_ref, raw, factor, out_buf, sems, factor_sem):
    pieces, rows, _ = q_ref.shape
    for k in range(pieces):
        raw[k * rows : (k + 1) * rows, :] = q_ref[k]
    factor[...] = scale * jnp.dot(
        inv_ref[...],
        raw[...],
        precision=lax.Precision.HIGHEST,
        preferred_element_type=F32,
    )
    copies = [pltpu.make_async_copy(factor, factor_ref, factor_sem)]
    copies[0].start()
    high, low = parts_of(factor[...], 2)
    tall = jnp.concatenate([high, low, high, jnp.zeros_like(low)], axis=0)
    blocks = sems.shape[0]
    block = out_ref.shape[0] // blocks
    for i in range(blocks):
        span = pl.ds(i * block, block)
        merged = hi_ref[span, :].astype(F32) + lo_ref[span, :].astype(F32)
        out_buf[span, :] = (merged - dot(stack_ref[span, :], tall)).astype(BF16)
        copies.append(
            pltpu.make_async_copy(out_buf.at[span, :], out_ref.at[span, :], sems.at[i])
        )
        copies[-1].start()
    for copy in copies:
        copy.wait()


def residual_of(q_all, inverse, stack, hi, lo, replicas):
    rank = inverse.shape[0]
    cols = hi.shape[1]
    return pl.pallas_call(
        lambda *refs: residual_kernel(1.0 / replicas, *refs),
        in_specs=[VMEM] * 5,
        out_specs=[HBM, HBM],
        out_shape=[
            jax.ShapeDtypeStruct(hi.shape, BF16),
            jax.ShapeDtypeStruct((rank, cols), F32),
        ],
        scratch_shapes=[
            pltpu.VMEM((rank, cols), F32),
            pltpu.VMEM((rank, cols), F32),
            pltpu.VMEM(hi.shape, BF16),
            pltpu.SemaphoreType.DMA((8,)),
            pltpu.SemaphoreType.DMA,
        ],
        compiler_params=PARAMS,
        name="residual",
    )(q_all, inverse, stack, hi, lo)


def total_kernel(x_ref, *refs):
    out_ref = refs[-1]
    total = x_ref[0]
    for s in range(1, x_ref.shape[0]):
        total = total + x_ref[s]
    for s in range(out_ref.shape[0]):
        out_ref[s] = total


def total_for(x, n, *after):
    return pl.pallas_call(
        total_kernel,
        in_specs=[VMEM] + [ANY] * len(after),
        out_specs=VMEM,
        out_shape=jax.ShapeDtypeStruct((n,) + x.shape[1:], F32),
        compiler_params=PARAMS,
        cost_estimate=cost(x.size, 4 * x.size),
        name="total",
    )(x, *after)


def per_device(acts, grads_out, error_buffer, prior_q):
    tensor = lax.axis_size("tensor")
    replicas = lax.axis_size("dp")
    side = math.isqrt(replicas)
    along_y = [[y * side + z for y in range(side)] for z in range(side)]
    along_z = [[y * side + z for z in range(side)] for y in range(side)]

    def over_tensor(x):
        return lax.all_to_all(x, "tensor", 0, 0)

    def over_y(x):
        return lax.all_to_all(x, "dp", 0, 0, axis_index_groups=along_y)

    def over_z(x):
        return lax.all_to_all(x, "dp", 0, 0, axis_index_groups=along_z)

    error = error_buffer[0]
    q_t = prior_q.T
    acts_all = lax.all_gather(acts, "tensor", axis=0, tiled=True)

    y_all = over_tensor(y_chunks(q_t, grads_out, tensor))
    p_terms = over_tensor(p_chunks(y_all, acts, error_term(q_t, error)))
    p_row = total_for(over_y(total_for(p_terms, side)), side)
    hi, lo = merged_parts(acts_all, grads_out, error, p_row)
    p_all = over_tensor(total_for(over_z(p_row), tensor, hi))

    pieces = q_pieces(p_all, hi, lo, side)
    q_sum = total_for(over_z(total_for(over_y(pieces), side)), side)
    q_all = over_y(q_sum)
    inverse, basis, stack = basis_of(p_all, q_sum)
    residual, factor = residual_of(q_all, inverse, stack, hi, lo, replicas)
    return (residual[None], basis.T, factor.T)


def solution(mesh):
    in_specs = (
        P(("dp", "tensor"), None),
        P("dp", "tensor"),
        P("dp", None, "tensor"),
        P("tensor", None),
    )
    out_specs = (P("dp", None, "tensor"), P(), P("tensor", None))
    return jax.shard_map(
        per_device, mesh=mesh, in_specs=in_specs, out_specs=out_specs, check_vma=False
    )
```

```python
import math

import jax
import jax.numpy as jnp
from jax import lax
from jax.experimental import pallas as pl
from jax.experimental.pallas import tpu as pltpu
from jax.sharding import PartitionSpec as P

F32 = jnp.float32
BF16 = jnp.bfloat16
VMEM = pl.BlockSpec(memory_space=pltpu.VMEM)
HBM = pl.BlockSpec(memory_space=pltpu.HBM)
ANY = pl.BlockSpec(memory_space=pl.ANY)
PARAMS = pltpu.CompilerParams(vmem_limit_bytes=32 * 1024 * 1024)
STREAM = pltpu.CompilerParams(vmem_limit_bytes=60 * 1024 * 1024)


def parts_of(x, n):
    out = []
    for _ in range(n):
        part = x.astype(BF16)
        out.append(part)
        x = x - part.astype(F32)
    return out


def dot(a, b, a_dim=1, b_dim=0):
    return lax.dot_general(
        a, b, (((a_dim,), (b_dim,)), ((), ())), preferred_element_type=F32
    )


def cost(flops, moved):
    return pl.CostEstimate(flops=flops, bytes_accessed=moved, transcendentals=0)


def y_kernel(q_ref, g_ref, out_ref, q_buf, g_buf, y_buf, q_sem, g_sems, y_sems):
    n, _, rows = out_ref.shape
    steps = g_sems.shape[0]
    block = g_ref.shape[0] // steps
    q_copy = pltpu.make_async_copy(q_ref, q_buf, q_sem)
    q_copy.start()
    loads, stores = [], []
    for i in range(steps):
        span = pl.ds(i * block, block)
        loads.append(
            pltpu.make_async_copy(g_ref.at[span, :], g_buf.at[span, :], g_sems.at[i])
        )
        loads[i].start()
    q_copy.wait()
    for i in range(steps):
        loads[i].wait()
        y = dot(q_buf[...], g_buf[i * block : (i + 1) * block, :], 1, 1)
        for k in range(block // rows):
            s = i * (block // rows) + k
            y_buf[s] = y[:, k * rows : (k + 1) * rows]
            stores.append(
                pltpu.make_async_copy(y_buf.at[s], out_ref.at[s], y_sems.at[s])
            )
            stores[s].start()
    for store in stores:
        store.wait()


def y_chunks(q_t, grads, n):
    rank, cols = q_t.shape
    rows = grads.shape[0] // n
    return pl.pallas_call(
        y_kernel,
        in_specs=[HBM, HBM],
        out_specs=HBM,
        out_shape=jax.ShapeDtypeStruct((n, rank, rows), F32),
        scratch_shapes=[
            pltpu.VMEM(q_t.shape, BF16),
            pltpu.VMEM(grads.shape, BF16),
            pltpu.VMEM((n, rank, rows), F32),
            pltpu.SemaphoreType.DMA,
            pltpu.SemaphoreType.DMA((2,)),
            pltpu.SemaphoreType.DMA((n,)),
        ],
        compiler_params=STREAM,
        cost_estimate=cost(2 * grads.size * rank * 8, grads.size * 2),
        name="y_chunks",
    )(q_t, grads)


def e_kernel(q_ref, e_ref, out_ref):
    out_ref[...] = dot(q_ref[...], e_ref[...], 1, 1)


def error_term(q_t, error):
    return pl.pallas_call(
        e_kernel,
        in_specs=[VMEM] * 2,
        out_specs=VMEM,
        out_shape=jax.ShapeDtypeStruct((q_t.shape[0], error.shape[0]), F32),
        compiler_params=PARAMS,
        cost_estimate=cost(2 * error.size * 32 * 8, error.size * 2),
        name="error_term",
    )(q_t, error)


def p_kernel(y_ref, acts_ref, e_ref, out_ref):
    n, rank, width = out_ref.shape
    y = y_ref[0]
    for s in range(1, n):
        y = y + y_ref[s]
    stack = jnp.concatenate(parts_of(y, 3), axis=0)
    p = dot(stack, acts_ref[...])
    p = (p[:rank] + e_ref[...]) + (p[rank : 2 * rank] + p[2 * rank :])
    for s in range(n):
        out_ref[s] = p[:, s * width : (s + 1) * width]


def p_chunks(y_all, acts, e_term):
    n, rank, _ = y_all.shape
    width = acts.shape[1] // n
    return pl.pallas_call(
        p_kernel,
        in_specs=[VMEM] * 3,
        out_specs=VMEM,
        out_shape=jax.ShapeDtypeStruct((n, rank, width), F32),
        compiler_params=PARAMS,
        cost_estimate=cost(2 * acts.size * rank * 8, acts.size * 2),
        name="p_chunks",
    )(y_all, acts, e_term)


def merged_kernel(a_ref, g_ref, e_ref, after_ref, hi_ref, lo_ref):
    del after_ref
    block = 256

    @pl.loop(0, a_ref.shape[1] // block)
    def _(i):
        span = pl.ds(pl.multiple_of(i * block, block), block)
        merged = dot(a_ref[:, span], g_ref[...], 0, 0) + e_ref[span, :].astype(F32)
        hi, lo = parts_of(merged, 2)
        hi_ref[span, :] = hi
        lo_ref[span, :] = lo


def merged_parts(acts_all, grads, error, after):
    tokens, width = acts_all.shape
    cols = grads.shape[1]
    shape = jax.ShapeDtypeStruct((width, cols), BF16)
    return pl.pallas_call(
        merged_kernel,
        in_specs=[VMEM, VMEM, VMEM, ANY],
        out_specs=[VMEM, VMEM],
        out_shape=[shape, shape],
        compiler_params=PARAMS,
        cost_estimate=cost(2 * tokens * width * cols, acts_all.size * 2 + grads.size * 2),
        name="merged_parts",
    )(acts_all, grads, error, after)


def q_kernel(p_ref, hi_ref, lo_ref, out_ref):
    n, rank, width = p_ref.shape
    pieces, rows, _ = out_ref.shape
    total = None
    for s in range(n):
        high, low = parts_of(p_ref[s], 2)
        span = slice(s * width, (s + 1) * width)
        both = dot(jnp.concatenate([high, low], axis=0), hi_ref[span, :])
        term = both[:rank] + (both[rank:] + dot(high, lo_ref[span, :]))
        total = term if total is None else total + term
    for k in range(pieces):
        out_ref[k] = total[k * rows : (k + 1) * rows, :]


def q_pieces(p_all, hi, lo, pieces):
    n, rank, width = p_all.shape
    cols = hi.shape[1]
    return pl.pallas_call(
        q_kernel,
        in_specs=[VMEM] * 3,
        out_specs=VMEM,
        out_shape=jax.ShapeDtypeStruct((pieces, rank // pieces, cols), F32),
        compiler_params=PARAMS,
        cost_estimate=cost(2 * hi.size * rank * 8, hi.size * 4),
        name="q_pieces",
    )(p_all, hi, lo)


def basis_kernel(p_ref, after_ref, inv_ref, basis_ref, stack_ref, full_ref):
    del after_ref
    n, rank, width = p_ref.shape
    for s in range(n):
        full_ref[:, s * width : (s + 1) * width] = p_ref[s]
    p = full_ref[...]
    gram = lax.dot_general(
        p,
        p,
        (((1,), (1,)), ((), ())),
        precision=lax.Precision.HIGHEST,
        preferred_element_type=F32,
    )
    row = lax.broadcasted_iota(jnp.int32, (rank, rank), 0)
    col = lax.broadcasted_iota(jnp.int32, (rank, rank), 1)
    eye = (row == col).astype(F32)
    work = jnp.concatenate([gram, eye], axis=1)
    below = lax.broadcasted_iota(jnp.int32, (rank, 1), 0)
    for j in range(rank - 1):
        pivot = work[j : j + 1, :]
        factor = jnp.where(below > j, work[:, j : j + 1] / pivot[:, j : j + 1], 0.0)
        work = work - factor * pivot
    upper = work[:, :rank]
    pivots = jnp.sum(jnp.where(row == col, upper, 0.0), axis=1, keepdims=True)
    inverse = work[:, rank:] / jnp.sqrt(pivots)
    inv_ref[...] = inverse
    basis = jnp.dot(
        inverse, p, precision=lax.Precision.HIGHEST, preferred_element_type=F32
    )
    basis_ref[...] = basis
    high = basis.astype(BF16).astype(F32)
    low = basis - high
    wide = jnp.concatenate([high, high, low, jnp.zeros_like(low)], axis=0)
    stack_ref[...] = wide.T.astype(BF16)


def basis_of(p_all, after):
    n, rank, width = p_all.shape
    size = n * width
    return pl.pallas_call(
        basis_kernel,
        in_specs=[VMEM, ANY],
        out_specs=[VMEM] * 3,
        out_shape=[
            jax.ShapeDtypeStruct((rank, rank), F32),
            jax.ShapeDtypeStruct((rank, size), F32),
            jax.ShapeDtypeStruct((size, 4 * rank), BF16),
        ],
        scratch_shapes=[pltpu.VMEM((rank, size), F32)],
        compiler_params=PARAMS,
        cost_estimate=cost(4_000_000_000, 4_000_000),
        name="basis",
    )(p_all, after)


def residual_kernel(scale, q_ref, inv_ref, stack_ref, hi_ref, lo_ref, out_ref, factor_ref, raw, factor, out_buf, sems, factor_sem):
    pieces, rows, _ = q_ref.shape
    for k in range(pieces):
        raw[k * rows : (k + 1) * rows, :] = q_ref[k]
    factor[...] = scale * jnp.dot(
        inv_ref[...],
        raw[...],
        precision=lax.Precision.HIGHEST,
        preferred_element_type=F32,
    )
    copies = [pltpu.make_async_copy(factor, factor_ref, factor_sem)]
    copies[0].start()
    high, low = parts_of(factor[...], 2)
    tall = jnp.concatenate([high, low, high, jnp.zeros_like(low)], axis=0)
    blocks = sems.shape[0]
    block = out_ref.shape[0] // blocks
    for i in range(blocks):
        span = pl.ds(i * block, block)
        merged = hi_ref[span, :].astype(F32) + lo_ref[span, :].astype(F32)
        out_buf[span, :] = (merged - dot(stack_ref[span, :], tall)).astype(BF16)
        copies.append(
            pltpu.make_async_copy(out_buf.at[span, :], out_ref.at[span, :], sems.at[i])
        )
        copies[-1].start()
    for copy in copies:
        copy.wait()


def residual_of(q_all, inverse, stack, hi, lo, replicas):
    rank = inverse.shape[0]
    cols = hi.shape[1]
    return pl.pallas_call(
        lambda *refs: residual_kernel(1.0 / replicas, *refs),
        in_specs=[VMEM] * 5,
        out_specs=[HBM, HBM],
        out_shape=[
            jax.ShapeDtypeStruct(hi.shape, BF16),
            jax.ShapeDtypeStruct((rank, cols), F32),
        ],
        scratch_shapes=[
            pltpu.VMEM((rank, cols), F32),
            pltpu.VMEM((rank, cols), F32),
            pltpu.VMEM(hi.shape, BF16),
            pltpu.SemaphoreType.DMA((8,)),
            pltpu.SemaphoreType.DMA,
        ],
        compiler_params=PARAMS,
        name="residual",
    )(q_all, inverse, stack, hi, lo)


def total_kernel(x_ref, out_ref):
    total = x_ref[0]
    for s in range(1, x_ref.shape[0]):
        total = total + x_ref[s]
    for s in range(out_ref.shape[0]):
        out_ref[s] = total


def total_for(x, n):
    return pl.pallas_call(
        total_kernel,
        in_specs=[VMEM],
        out_specs=VMEM,
        out_shape=jax.ShapeDtypeStruct((n,) + x.shape[1:], F32),
        compiler_params=PARAMS,
        cost_estimate=cost(x.size, 4 * x.size),
        name="total",
    )(x)


def per_device(acts, grads_out, error_buffer, prior_q):
    tensor = lax.axis_size("tensor")
    replicas = lax.axis_size("dp")
    side = math.isqrt(replicas)
    along_y = [[y * side + z for y in range(side)] for z in range(side)]
    along_z = [[y * side + z for z in range(side)] for y in range(side)]

    def over_tensor(x):
        return lax.all_to_all(x, "tensor", 0, 0)

    def over_y(x):
        return lax.all_to_all(x, "dp", 0, 0, axis_index_groups=along_y)

    def over_z(x):
        return lax.all_to_all(x, "dp", 0, 0, axis_index_groups=along_z)

    error = error_buffer[0]
    q_t = prior_q.T
    acts_all = lax.all_gather(acts, "tensor", axis=0, tiled=True)

    y_all = over_tensor(y_chunks(q_t, grads_out, tensor))
    p_terms = over_tensor(p_chunks(y_all, acts, error_term(q_t, error)))
    p_row = total_for(over_y(total_for(p_terms, side)), side)
    p_last = total_for(over_z(p_row), tensor)
    p_all = over_tensor(p_last)
    hi, lo = merged_parts(acts_all, grads_out, error, p_last)

    pieces = q_pieces(p_all, hi, lo, side)
    q_sum = total_for(over_z(total_for(over_y(pieces), side)), side)
    q_all = over_y(q_sum)
    inverse, basis, stack = basis_of(p_all, q_sum)
    residual, factor = residual_of(q_all, inverse, stack, hi, lo, replicas)
    return (residual[None], basis.T, factor.T)


def solution(mesh):
    in_specs = (
        P(("dp", "tensor"), None),
        P("dp", "tensor"),
        P("dp", None, "tensor"),
        P("tensor", None),
    )
    out_specs = (P("dp", None, "tensor"), P(), P("tensor", None))
    return jax.shard_map(
        per_device, mesh=mesh, in_specs=in_specs, out_specs=out_specs, check_vma=False
    )
```

```python
import math

import jax
import jax.numpy as jnp
from jax import lax
from jax.experimental import pallas as pl
from jax.experimental.pallas import tpu as pltpu
from jax.sharding import PartitionSpec as P

F32 = jnp.float32
BF16 = jnp.bfloat16
VMEM = pl.BlockSpec(memory_space=pltpu.VMEM)
HBM = pl.BlockSpec(memory_space=pltpu.HBM)
ANY = pl.BlockSpec(memory_space=pl.ANY)
PARAMS = pltpu.CompilerParams(vmem_limit_bytes=32 * 1024 * 1024)
STREAM = pltpu.CompilerParams(vmem_limit_bytes=60 * 1024 * 1024)


def parts_of(x, n):
    out = []
    for _ in range(n):
        part = x.astype(BF16)
        out.append(part)
        x = x - part.astype(F32)
    return out


def dot(a, b, a_dim=1, b_dim=0):
    return lax.dot_general(
        a, b, (((a_dim,), (b_dim,)), ((), ())), preferred_element_type=F32
    )


def cost(flops, moved):
    return pl.CostEstimate(flops=flops, bytes_accessed=moved, transcendentals=0)


def y_kernel(q_ref, g_ref, out_ref, q_buf, g_buf, y_buf, q_sem, g_sems, y_sems):
    n, _, rows = out_ref.shape
    steps = g_sems.shape[0]
    block = g_ref.shape[0] // steps
    q_copy = pltpu.make_async_copy(q_ref, q_buf, q_sem)
    q_copy.start()
    loads, stores = [], []
    for i in range(steps):
        span = pl.ds(i * block, block)
        loads.append(
            pltpu.make_async_copy(g_ref.at[span, :], g_buf.at[span, :], g_sems.at[i])
        )
        loads[i].start()
    q_copy.wait()
    for i in range(steps):
        loads[i].wait()
        y = dot(q_buf[...], g_buf[i * block : (i + 1) * block, :], 1, 1)
        for k in range(block // rows):
            s = i * (block // rows) + k
            y_buf[s] = y[:, k * rows : (k + 1) * rows]
            stores.append(
                pltpu.make_async_copy(y_buf.at[s], out_ref.at[s], y_sems.at[s])
            )
            stores[s].start()
    for store in stores:
        store.wait()


def y_chunks(q_t, grads, n):
    rank, cols = q_t.shape
    rows = grads.shape[0] // n
    return pl.pallas_call(
        y_kernel,
        in_specs=[HBM, HBM],
        out_specs=HBM,
        out_shape=jax.ShapeDtypeStruct((n, rank, rows), F32),
        scratch_shapes=[
            pltpu.VMEM(q_t.shape, BF16),
            pltpu.VMEM(grads.shape, BF16),
            pltpu.VMEM((n, rank, rows), F32),
            pltpu.SemaphoreType.DMA,
            pltpu.SemaphoreType.DMA((2,)),
            pltpu.SemaphoreType.DMA((n,)),
        ],
        compiler_params=STREAM,
        cost_estimate=cost(2 * grads.size * rank * 8, grads.size * 2),
        name="y_chunks",
    )(q_t, grads)


def e_kernel(q_ref, e_ref, out_ref):
    out_ref[...] = dot(q_ref[...], e_ref[...], 1, 1)


def error_term(q_t, error):
    return pl.pallas_call(
        e_kernel,
        in_specs=[VMEM] * 2,
        out_specs=VMEM,
        out_shape=jax.ShapeDtypeStruct((q_t.shape[0], error.shape[0]), F32),
        compiler_params=PARAMS,
        cost_estimate=cost(2 * error.size * 32 * 8, error.size * 2),
        name="error_term",
    )(q_t, error)


def p_kernel(y_ref, acts_ref, e_ref, out_ref):
    n, rank, width = out_ref.shape
    y = y_ref[0]
    for s in range(1, n):
        y = y + y_ref[s]
    stack = jnp.concatenate(parts_of(y, 3), axis=0)
    p = dot(stack, acts_ref[...])
    p = (p[:rank] + e_ref[...]) + (p[rank : 2 * rank] + p[2 * rank :])
    for s in range(n):
        out_ref[s] = p[:, s * width : (s + 1) * width]


def p_chunks(y_all, acts, e_term):
    n, rank, _ = y_all.shape
    width = acts.shape[1] // n
    return pl.pallas_call(
        p_kernel,
        in_specs=[VMEM] * 3,
        out_specs=VMEM,
        out_shape=jax.ShapeDtypeStruct((n, rank, width), F32),
        compiler_params=PARAMS,
        cost_estimate=cost(2 * acts.size * rank * 8, acts.size * 2),
        name="p_chunks",
    )(y_all, acts, e_term)


def merged_kernel(a_ref, g_ref, e_ref, after_ref, hi_ref, lo_ref, a_buf, g_buf, e_buf, a_sems, g_sem, e_sem):
    del after_ref
    blocks, _, block = a_buf.shape

    def load(i):
        span = pl.ds(pl.multiple_of(i * block, block), block)
        return pltpu.make_async_copy(a_ref.at[:, span], a_buf.at[i], a_sems.at[i])

    g_load = pltpu.make_async_copy(g_ref, g_buf, g_sem)
    e_load = pltpu.make_async_copy(e_ref, e_buf, e_sem)
    g_load.start()
    load(0).start()
    e_load.start()
    for i in range(1, blocks):
        load(i).start()
    g_load.wait()

    @pl.loop(0, blocks)
    def _(i):
        load(i).wait()
        grad = dot(a_buf[i], g_buf[...], 0, 0)

        @pl.when(i == 0)
        def _():
            e_load.wait()

        span = pl.ds(pl.multiple_of(i * block, block), block)
        hi, lo = parts_of(grad + e_buf[span, :].astype(F32), 2)
        hi_ref[span, :] = hi
        lo_ref[span, :] = lo


def merged_parts(acts_all, grads, error, after):
    tokens, width = acts_all.shape
    cols = grads.shape[1]
    block = 256
    blocks = width // block
    shape = jax.ShapeDtypeStruct((width, cols), BF16)
    streamed = [
        pltpu.with_memory_space_constraint(x, pltpu.HBM)
        for x in (acts_all, grads, error)
    ]
    return pl.pallas_call(
        merged_kernel,
        in_specs=[HBM, HBM, HBM, ANY],
        out_specs=[VMEM, VMEM],
        out_shape=[shape, shape],
        scratch_shapes=[
            pltpu.VMEM((blocks, tokens, block), BF16),
            pltpu.VMEM(grads.shape, BF16),
            pltpu.VMEM(error.shape, BF16),
            pltpu.SemaphoreType.DMA((blocks,)),
            pltpu.SemaphoreType.DMA,
            pltpu.SemaphoreType.DMA,
        ],
        compiler_params=PARAMS,
        cost_estimate=cost(2 * tokens * width * cols, acts_all.size * 2 + grads.size * 2),
        name="merged_parts",
    )(*streamed, after)


def q_kernel(p_ref, hi_ref, lo_ref, out_ref):
    n, rank, width = p_ref.shape
    pieces, rows, _ = out_ref.shape
    total = None
    for s in range(n):
        high, low = parts_of(p_ref[s], 2)
        span = slice(s * width, (s + 1) * width)
        both = dot(jnp.concatenate([high, low], axis=0), hi_ref[span, :])
        term = both[:rank] + (both[rank:] + dot(high, lo_ref[span, :]))
        total = term if total is None else total + term
    for k in range(pieces):
        out_ref[k] = total[k * rows : (k + 1) * rows, :]


def q_pieces(p_all, hi, lo, pieces):
    n, rank, width = p_all.shape
    cols = hi.shape[1]
    return pl.pallas_call(
        q_kernel,
        in_specs=[VMEM] * 3,
        out_specs=VMEM,
        out_shape=jax.ShapeDtypeStruct((pieces, rank // pieces, cols), F32),
        compiler_params=PARAMS,
        cost_estimate=cost(2 * hi.size * rank * 8, hi.size * 4),
        name="q_pieces",
    )(p_all, hi, lo)


def basis_kernel(p_ref, after_ref, inv_ref, basis_ref, stack_ref, full_ref):
    del after_ref
    n, rank, width = p_ref.shape
    for s in range(n):
        full_ref[:, s * width : (s + 1) * width] = p_ref[s]
    p = full_ref[...]
    gram = lax.dot_general(
        p,
        p,
        (((1,), (1,)), ((), ())),
        precision=lax.Precision.HIGHEST,
        preferred_element_type=F32,
    )
    row = lax.broadcasted_iota(jnp.int32, (rank, rank), 0)
    col = lax.broadcasted_iota(jnp.int32, (rank, rank), 1)
    eye = (row == col).astype(F32)
    work = jnp.concatenate([gram, eye], axis=1)
    below = lax.broadcasted_iota(jnp.int32, (rank, 1), 0)
    for j in range(rank - 1):
        pivot = work[j : j + 1, :]
        factor = jnp.where(below > j, work[:, j : j + 1] / pivot[:, j : j + 1], 0.0)
        work = work - factor * pivot
    upper = work[:, :rank]
    pivots = jnp.sum(jnp.where(row == col, upper, 0.0), axis=1, keepdims=True)
    inverse = work[:, rank:] / jnp.sqrt(pivots)
    inv_ref[...] = inverse
    basis = jnp.dot(
        inverse, p, precision=lax.Precision.HIGHEST, preferred_element_type=F32
    )
    basis_ref[...] = basis
    high = basis.astype(BF16).astype(F32)
    low = basis - high
    wide = jnp.concatenate([high, high, low, jnp.zeros_like(low)], axis=0)
    stack_ref[...] = wide.T.astype(BF16)


def basis_of(p_all, after):
    n, rank, width = p_all.shape
    size = n * width
    return pl.pallas_call(
        basis_kernel,
        in_specs=[VMEM, ANY],
        out_specs=[VMEM] * 3,
        out_shape=[
            jax.ShapeDtypeStruct((rank, rank), F32),
            jax.ShapeDtypeStruct((rank, size), F32),
            jax.ShapeDtypeStruct((size, 4 * rank), BF16),
        ],
        scratch_shapes=[pltpu.VMEM((rank, size), F32)],
        compiler_params=PARAMS,
        cost_estimate=cost(4_000_000_000, 4_000_000),
        name="basis",
    )(p_all, after)


def residual_kernel(scale, q_ref, inv_ref, stack_ref, hi_ref, lo_ref, out_ref, factor_ref, raw, factor, out_buf, sems, factor_sem):
    pieces, rows, _ = q_ref.shape
    for k in range(pieces):
        raw[k * rows : (k + 1) * rows, :] = q_ref[k]
    factor[...] = scale * jnp.dot(
        inv_ref[...],
        raw[...],
        precision=lax.Precision.HIGHEST,
        preferred_element_type=F32,
    )
    copies = [pltpu.make_async_copy(factor, factor_ref, factor_sem)]
    copies[0].start()
    high, low = parts_of(factor[...], 2)
    tall = jnp.concatenate([high, low, high, jnp.zeros_like(low)], axis=0)
    blocks = sems.shape[0]
    block = out_ref.shape[0] // blocks
    for i in range(blocks):
        span = pl.ds(i * block, block)
        merged = hi_ref[span, :].astype(F32) + lo_ref[span, :].astype(F32)
        out_buf[span, :] = (merged - dot(stack_ref[span, :], tall)).astype(BF16)
        copies.append(
            pltpu.make_async_copy(out_buf.at[span, :], out_ref.at[span, :], sems.at[i])
        )
        copies[-1].start()
    for copy in copies:
        copy.wait()


def residual_of(q_all, inverse, stack, hi, lo, replicas):
    rank = inverse.shape[0]
    cols = hi.shape[1]
    return pl.pallas_call(
        lambda *refs: residual_kernel(1.0 / replicas, *refs),
        in_specs=[VMEM] * 5,
        out_specs=[HBM, HBM],
        out_shape=[
            jax.ShapeDtypeStruct(hi.shape, BF16),
            jax.ShapeDtypeStruct((rank, cols), F32),
        ],
        scratch_shapes=[
            pltpu.VMEM((rank, cols), F32),
            pltpu.VMEM((rank, cols), F32),
            pltpu.VMEM(hi.shape, BF16),
            pltpu.SemaphoreType.DMA((8,)),
            pltpu.SemaphoreType.DMA,
        ],
        compiler_params=PARAMS,
        name="residual",
    )(q_all, inverse, stack, hi, lo)


def total_kernel(x_ref, out_ref):
    total = x_ref[0]
    for s in range(1, x_ref.shape[0]):
        total = total + x_ref[s]
    for s in range(out_ref.shape[0]):
        out_ref[s] = total


def total_for(x, n):
    return pl.pallas_call(
        total_kernel,
        in_specs=[VMEM],
        out_specs=VMEM,
        out_shape=jax.ShapeDtypeStruct((n,) + x.shape[1:], F32),
        compiler_params=PARAMS,
        cost_estimate=cost(x.size, 4 * x.size),
        name="total",
    )(x)


def per_device(acts, grads_out, error_buffer, prior_q):
    tensor = lax.axis_size("tensor")
    replicas = lax.axis_size("dp")
    side = math.isqrt(replicas)
    along_y = [[y * side + z for y in range(side)] for z in range(side)]
    along_z = [[y * side + z for z in range(side)] for y in range(side)]

    def over_tensor(x):
        return lax.all_to_all(x, "tensor", 0, 0)

    def over_y(x):
        return lax.all_to_all(x, "dp", 0, 0, axis_index_groups=along_y)

    def over_z(x):
        return lax.all_to_all(x, "dp", 0, 0, axis_index_groups=along_z)

    error = error_buffer[0]
    q_t = prior_q.T
    acts_all = lax.all_gather(acts, "tensor", axis=0, tiled=True)

    y_all = over_tensor(y_chunks(q_t, grads_out, tensor))
    p_terms = over_tensor(p_chunks(y_all, acts, error_term(q_t, error)))
    p_row = total_for(over_y(total_for(p_terms, side)), side)
    p_last = total_for(over_z(p_row), tensor)
    p_all = over_tensor(p_last)
    hi, lo = merged_parts(acts_all, grads_out, error, p_last)

    pieces = q_pieces(p_all, hi, lo, side)
    q_sum = total_for(over_z(total_for(over_y(pieces), side)), side)
    q_all = over_y(q_sum)
    inverse, basis, stack = basis_of(p_all, q_sum)
    residual, factor = residual_of(q_all, inverse, stack, hi, lo, replicas)
    return (residual[None], basis.T, factor.T)


def solution(mesh):
    in_specs = (
        P(("dp", "tensor"), None),
        P("dp", "tensor"),
        P("dp", None, "tensor"),
        P("tensor", None),
    )
    out_specs = (P("dp", None, "tensor"), P(), P("tensor", None))
    return jax.shard_map(
        per_device, mesh=mesh, in_specs=in_specs, out_specs=out_specs, check_vma=False
    )
```

```python
import math

import jax
import jax.numpy as jnp
from jax import lax
from jax.experimental import pallas as pl
from jax.experimental.pallas import tpu as pltpu
from jax.sharding import PartitionSpec as P

F32 = jnp.float32
BF16 = jnp.bfloat16
VMEM = pl.BlockSpec(memory_space=pltpu.VMEM)
HBM = pl.BlockSpec(memory_space=pltpu.HBM)
ANY = pl.BlockSpec(memory_space=pl.ANY)
PARAMS = pltpu.CompilerParams(vmem_limit_bytes=32 * 1024 * 1024)
STREAM = pltpu.CompilerParams(vmem_limit_bytes=60 * 1024 * 1024)


def parts_of(x, n):
    out = []
    for _ in range(n):
        part = x.astype(BF16)
        out.append(part)
        x = x - part.astype(F32)
    return out


def dot(a, b, a_dim=1, b_dim=0):
    return lax.dot_general(
        a, b, (((a_dim,), (b_dim,)), ((), ())), preferred_element_type=F32
    )


def cost(flops, moved):
    return pl.CostEstimate(flops=flops, bytes_accessed=moved, transcendentals=0)


def y_kernel(q_ref, g_ref, out_ref, q_buf, g_buf, y_buf, q_sem, g_sems, y_sems):
    n, _, rows = out_ref.shape
    steps = g_sems.shape[0]
    block = g_ref.shape[0] // steps
    q_copy = pltpu.make_async_copy(q_ref, q_buf, q_sem)
    q_copy.start()
    loads, stores = [], []
    for i in range(steps):
        span = pl.ds(i * block, block)
        loads.append(
            pltpu.make_async_copy(g_ref.at[span, :], g_buf.at[span, :], g_sems.at[i])
        )
        loads[i].start()
    q_copy.wait()
    for i in range(steps):
        loads[i].wait()
        y = dot(q_buf[...], g_buf[i * block : (i + 1) * block, :], 1, 1)
        for k in range(block // rows):
            s = i * (block // rows) + k
            y_buf[s] = y[:, k * rows : (k + 1) * rows]
            stores.append(
                pltpu.make_async_copy(y_buf.at[s], out_ref.at[s], y_sems.at[s])
            )
            stores[s].start()
    for store in stores:
        store.wait()


def y_chunks(q_t, grads, n):
    rank, cols = q_t.shape
    rows = grads.shape[0] // n
    return pl.pallas_call(
        y_kernel,
        in_specs=[HBM, HBM],
        out_specs=HBM,
        out_shape=jax.ShapeDtypeStruct((n, rank, rows), F32),
        scratch_shapes=[
            pltpu.VMEM(q_t.shape, BF16),
            pltpu.VMEM(grads.shape, BF16),
            pltpu.VMEM((n, rank, rows), F32),
            pltpu.SemaphoreType.DMA,
            pltpu.SemaphoreType.DMA((2,)),
            pltpu.SemaphoreType.DMA((n,)),
        ],
        compiler_params=STREAM,
        cost_estimate=cost(2 * grads.size * rank * 8, grads.size * 2),
        name="y_chunks",
    )(q_t, grads)


def e_kernel(q_ref, e_ref, out_ref):
    out_ref[...] = dot(q_ref[...], e_ref[...], 1, 1)


def error_term(q_t, error):
    return pl.pallas_call(
        e_kernel,
        in_specs=[VMEM] * 2,
        out_specs=VMEM,
        out_shape=jax.ShapeDtypeStruct((q_t.shape[0], error.shape[0]), F32),
        compiler_params=PARAMS,
        cost_estimate=cost(2 * error.size * 32 * 8, error.size * 2),
        name="error_term",
    )(q_t, error)


def p_kernel(y_ref, acts_ref, e_ref, out_ref):
    n, rank, width = out_ref.shape
    y = y_ref[0]
    for s in range(1, n):
        y = y + y_ref[s]
    stack = jnp.concatenate(parts_of(y, 3), axis=0)
    p = dot(stack, acts_ref[...])
    p = (p[:rank] + e_ref[...]) + (p[rank : 2 * rank] + p[2 * rank :])
    for s in range(n):
        out_ref[s] = p[:, s * width : (s + 1) * width]


def p_chunks(y_all, acts, e_term):
    n, rank, _ = y_all.shape
    width = acts.shape[1] // n
    return pl.pallas_call(
        p_kernel,
        in_specs=[VMEM] * 3,
        out_specs=VMEM,
        out_shape=jax.ShapeDtypeStruct((n, rank, width), F32),
        compiler_params=PARAMS,
        cost_estimate=cost(2 * acts.size * rank * 8, acts.size * 2),
        name="p_chunks",
    )(y_all, acts, e_term)


def merged_kernel(a_ref, g_ref, e_ref, after_ref, hi_ref, lo_ref, a_buf, e_buf, a_sems, e_sems):
    del after_ref
    blocks, _, block = a_buf.shape

    def loads(i):
        span = pl.ds(i * block, block)
        return (
            pltpu.make_async_copy(a_ref.at[:, span], a_buf.at[i], a_sems.at[i]),
            pltpu.make_async_copy(e_ref.at[span, :], e_buf.at[i], e_sems.at[i]),
        )

    for load in loads(0):
        load.start()
    for i in range(blocks):
        for load in loads(i):
            load.wait()
        if i + 1 < blocks:
            for load in loads(i + 1):
                load.start()
        merged = dot(a_buf[i], g_ref[...], 0, 0) + e_buf[i].astype(F32)
        hi, lo = parts_of(merged, 2)
        span = slice(i * block, (i + 1) * block)
        hi_ref[span, :] = hi
        lo_ref[span, :] = lo


def merged_parts(acts_all, grads, error, after):
    tokens, width = acts_all.shape
    cols = grads.shape[1]
    blocks = 2
    block = width // blocks
    shape = jax.ShapeDtypeStruct((width, cols), BF16)
    return pl.pallas_call(
        merged_kernel,
        in_specs=[HBM, VMEM, HBM, ANY],
        out_specs=[VMEM, VMEM],
        out_shape=[shape, shape],
        scratch_shapes=[
            pltpu.VMEM((blocks, tokens, block), BF16),
            pltpu.VMEM((blocks, block, cols), BF16),
            pltpu.SemaphoreType.DMA((blocks,)),
            pltpu.SemaphoreType.DMA((blocks,)),
        ],
        compiler_params=PARAMS,
        cost_estimate=cost(2 * tokens * width * cols, acts_all.size * 2 + grads.size * 2),
        name="merged_parts",
    )(
        pltpu.with_memory_space_constraint(acts_all, pltpu.HBM),
        grads,
        pltpu.with_memory_space_constraint(error, pltpu.HBM),
        after,
    )


def q_kernel(p_ref, hi_ref, lo_ref, out_ref):
    n, rank, width = p_ref.shape
    pieces, rows, _ = out_ref.shape
    total = None
    for s in range(n):
        high, low = parts_of(p_ref[s], 2)
        span = slice(s * width, (s + 1) * width)
        both = dot(jnp.concatenate([high, low], axis=0), hi_ref[span, :])
        term = both[:rank] + (both[rank:] + dot(high, lo_ref[span, :]))
        total = term if total is None else total + term
    for k in range(pieces):
        out_ref[k] = total[k * rows : (k + 1) * rows, :]


def q_pieces(p_all, hi, lo, pieces):
    n, rank, width = p_all.shape
    cols = hi.shape[1]
    return pl.pallas_call(
        q_kernel,
        in_specs=[VMEM] * 3,
        out_specs=VMEM,
        out_shape=jax.ShapeDtypeStruct((pieces, rank // pieces, cols), F32),
        compiler_params=PARAMS,
        cost_estimate=cost(2 * hi.size * rank * 8, hi.size * 4),
        name="q_pieces",
    )(p_all, hi, lo)


def basis_kernel(p_ref, after_ref, inv_ref, basis_ref, stack_ref, full_ref):
    del after_ref
    n, rank, width = p_ref.shape
    for s in range(n):
        full_ref[:, s * width : (s + 1) * width] = p_ref[s]
    p = full_ref[...]
    gram = lax.dot_general(
        p,
        p,
        (((1,), (1,)), ((), ())),
        precision=lax.Precision.HIGHEST,
        preferred_element_type=F32,
    )
    row = lax.broadcasted_iota(jnp.int32, (rank, rank), 0)
    col = lax.broadcasted_iota(jnp.int32, (rank, rank), 1)
    eye = (row == col).astype(F32)
    work = jnp.concatenate([gram, eye], axis=1)
    below = lax.broadcasted_iota(jnp.int32, (rank, 1), 0)
    for j in range(rank - 1):
        pivot = work[j : j + 1, :]
        factor = jnp.where(below > j, work[:, j : j + 1] / pivot[:, j : j + 1], 0.0)
        work = work - factor * pivot
    upper = work[:, :rank]
    pivots = jnp.sum(jnp.where(row == col, upper, 0.0), axis=1, keepdims=True)
    inverse = work[:, rank:] / jnp.sqrt(pivots)
    inv_ref[...] = inverse
    basis = jnp.dot(
        inverse, p, precision=lax.Precision.HIGHEST, preferred_element_type=F32
    )
    basis_ref[...] = basis
    high = basis.astype(BF16).astype(F32)
    low = basis - high
    wide = jnp.concatenate([high, high, low, jnp.zeros_like(low)], axis=0)
    stack_ref[...] = wide.T.astype(BF16)


def basis_of(p_all, after):
    n, rank, width = p_all.shape
    size = n * width
    return pl.pallas_call(
        basis_kernel,
        in_specs=[VMEM, ANY],
        out_specs=[VMEM] * 3,
        out_shape=[
            jax.ShapeDtypeStruct((rank, rank), F32),
            jax.ShapeDtypeStruct((rank, size), F32),
            jax.ShapeDtypeStruct((size, 4 * rank), BF16),
        ],
        scratch_shapes=[pltpu.VMEM((rank, size), F32)],
        compiler_params=PARAMS,
        cost_estimate=cost(4_000_000_000, 4_000_000),
        name="basis",
    )(p_all, after)


def residual_kernel(scale, q_ref, inv_ref, stack_ref, hi_ref, lo_ref, out_ref, factor_ref, raw, factor, out_buf, sems, factor_sem):
    pieces, rows, _ = q_ref.shape
    for k in range(pieces):
        raw[k * rows : (k + 1) * rows, :] = q_ref[k]
    factor[...] = scale * jnp.dot(
        inv_ref[...],
        raw[...],
        precision=lax.Precision.HIGHEST,
        preferred_element_type=F32,
    )
    copies = [pltpu.make_async_copy(factor, factor_ref, factor_sem)]
    copies[0].start()
    high, low = parts_of(factor[...], 2)
    tall = jnp.concatenate([high, low, high, jnp.zeros_like(low)], axis=0)
    blocks = sems.shape[0]
    block = out_ref.shape[0] // blocks
    for i in range(blocks):
        span = pl.ds(i * block, block)
        merged = hi_ref[span, :].astype(F32) + lo_ref[span, :].astype(F32)
        out_buf[span, :] = (merged - dot(stack_ref[span, :], tall)).astype(BF16)
        copies.append(
            pltpu.make_async_copy(out_buf.at[span, :], out_ref.at[span, :], sems.at[i])
        )
        copies[-1].start()
    for copy in copies:
        copy.wait()


def residual_of(q_all, inverse, stack, hi, lo, replicas):
    rank = inverse.shape[0]
    cols = hi.shape[1]
    return pl.pallas_call(
        lambda *refs: residual_kernel(1.0 / replicas, *refs),
        in_specs=[VMEM] * 5,
        out_specs=[HBM, HBM],
        out_shape=[
            jax.ShapeDtypeStruct(hi.shape, BF16),
            jax.ShapeDtypeStruct((rank, cols), F32),
        ],
        scratch_shapes=[
            pltpu.VMEM((rank, cols), F32),
            pltpu.VMEM((rank, cols), F32),
            pltpu.VMEM(hi.shape, BF16),
            pltpu.SemaphoreType.DMA((8,)),
            pltpu.SemaphoreType.DMA,
        ],
        compiler_params=PARAMS,
        name="residual",
    )(q_all, inverse, stack, hi, lo)


def total_kernel(x_ref, out_ref):
    total = x_ref[0]
    for s in range(1, x_ref.shape[0]):
        total = total + x_ref[s]
    for s in range(out_ref.shape[0]):
        out_ref[s] = total


def total_for(x, n):
    return pl.pallas_call(
        total_kernel,
        in_specs=[VMEM],
        out_specs=VMEM,
        out_shape=jax.ShapeDtypeStruct((n,) + x.shape[1:], F32),
        compiler_params=PARAMS,
        cost_estimate=cost(x.size, 4 * x.size),
        name="total",
    )(x)


def per_device(acts, grads_out, error_buffer, prior_q):
    tensor = lax.axis_size("tensor")
    replicas = lax.axis_size("dp")
    side = math.isqrt(replicas)
    along_y = [[y * side + z for y in range(side)] for z in range(side)]
    along_z = [[y * side + z for z in range(side)] for y in range(side)]

    def over_tensor(x):
        return lax.all_to_all(x, "tensor", 0, 0)

    def over_y(x):
        return lax.all_to_all(x, "dp", 0, 0, axis_index_groups=along_y)

    def over_z(x):
        return lax.all_to_all(x, "dp", 0, 0, axis_index_groups=along_z)

    error = error_buffer[0]
    q_t = prior_q.T
    acts_all = lax.all_gather(acts, "tensor", axis=0, tiled=True)

    y_all = over_tensor(y_chunks(q_t, grads_out, tensor))
    p_terms = over_tensor(p_chunks(y_all, acts, error_term(q_t, error)))
    p_row = total_for(over_y(total_for(p_terms, side)), side)
    p_last = total_for(over_z(p_row), tensor)
    p_all = over_tensor(p_last)
    hi, lo = merged_parts(acts_all, grads_out, error, p_last)

    pieces = q_pieces(p_all, hi, lo, side)
    q_sum = total_for(over_z(total_for(over_y(pieces), side)), side)
    q_all = over_y(q_sum)
    inverse, basis, stack = basis_of(p_all, q_sum)
    residual, factor = residual_of(q_all, inverse, stack, hi, lo, replicas)
    return (residual[None], basis.T, factor.T)


def solution(mesh):
    in_specs = (
        P(("dp", "tensor"), None),
        P("dp", "tensor"),
        P("dp", None, "tensor"),
        P("tensor", None),
    )
    out_specs = (P("dp", None, "tensor"), P(), P("tensor", None))
    return jax.shard_map(
        per_device, mesh=mesh, in_specs=in_specs, out_specs=out_specs, check_vma=False
    )
```

```python
import math

import jax
import jax.numpy as jnp
from jax import lax
from jax.experimental import pallas as pl
from jax.experimental.pallas import tpu as pltpu
from jax.sharding import PartitionSpec as P

F32 = jnp.float32
BF16 = jnp.bfloat16
VMEM = pl.BlockSpec(memory_space=pltpu.VMEM)
HBM = pl.BlockSpec(memory_space=pltpu.HBM)
ANY = pl.BlockSpec(memory_space=pl.ANY)
PARAMS = pltpu.CompilerParams(vmem_limit_bytes=32 * 1024 * 1024)
STREAM = pltpu.CompilerParams(vmem_limit_bytes=60 * 1024 * 1024)


def parts_of(x, n):
    out = []
    for _ in range(n):
        part = x.astype(BF16)
        out.append(part)
        x = x - part.astype(F32)
    return out


def dot(a, b, a_dim=1, b_dim=0):
    return lax.dot_general(
        a, b, (((a_dim,), (b_dim,)), ((), ())), preferred_element_type=F32
    )


def cost(flops, moved):
    return pl.CostEstimate(flops=flops, bytes_accessed=moved, transcendentals=0)


def y_kernel(q_ref, g_ref, out_ref, q_buf, g_buf, y_buf, q_sem, g_sems, y_sems):
    n, _, rows = out_ref.shape
    steps = g_sems.shape[0]
    block = g_ref.shape[0] // steps
    q_copy = pltpu.make_async_copy(q_ref, q_buf, q_sem)
    q_copy.start()
    loads, stores = [], []
    for i in range(steps):
        span = pl.ds(i * block, block)
        loads.append(
            pltpu.make_async_copy(g_ref.at[span, :], g_buf.at[span, :], g_sems.at[i])
        )
        loads[i].start()
    q_copy.wait()
    for i in range(steps):
        loads[i].wait()
        y = dot(q_buf[...], g_buf[i * block : (i + 1) * block, :], 1, 1)
        for k in range(block // rows):
            s = i * (block // rows) + k
            y_buf[s] = y[:, k * rows : (k + 1) * rows]
            stores.append(
                pltpu.make_async_copy(y_buf.at[s], out_ref.at[s], y_sems.at[s])
            )
            stores[s].start()
    for store in stores:
        store.wait()


def y_chunks(q_t, grads, n):
    rank, cols = q_t.shape
    rows = grads.shape[0] // n
    return pl.pallas_call(
        y_kernel,
        in_specs=[HBM, HBM],
        out_specs=HBM,
        out_shape=jax.ShapeDtypeStruct((n, rank, rows), F32),
        scratch_shapes=[
            pltpu.VMEM(q_t.shape, BF16),
            pltpu.VMEM(grads.shape, BF16),
            pltpu.VMEM((n, rank, rows), F32),
            pltpu.SemaphoreType.DMA,
            pltpu.SemaphoreType.DMA((2,)),
            pltpu.SemaphoreType.DMA((n,)),
        ],
        compiler_params=STREAM,
        cost_estimate=cost(2 * grads.size * rank * 8, grads.size * 2),
        name="y_chunks",
    )(q_t, grads)


def e_kernel(q_ref, e_ref, out_ref):
    out_ref[...] = dot(q_ref[...], e_ref[...], 1, 1)


def error_term(q_t, error):
    return pl.pallas_call(
        e_kernel,
        in_specs=[VMEM] * 2,
        out_specs=VMEM,
        out_shape=jax.ShapeDtypeStruct((q_t.shape[0], error.shape[0]), F32),
        compiler_params=PARAMS,
        cost_estimate=cost(2 * error.size * 32 * 8, error.size * 2),
        name="error_term",
    )(q_t, error)


def p_kernel(y_ref, acts_ref, e_ref, out_ref):
    n, rank, width = out_ref.shape
    y = y_ref[0]
    for s in range(1, n):
        y = y + y_ref[s]
    stack = jnp.concatenate(parts_of(y, 3), axis=0)
    p = dot(stack, acts_ref[...])
    p = (p[:rank] + e_ref[...]) + (p[rank : 2 * rank] + p[2 * rank :])
    for s in range(n):
        out_ref[s] = p[:, s * width : (s + 1) * width]


def p_chunks(y_all, acts, e_term):
    n, rank, _ = y_all.shape
    width = acts.shape[1] // n
    return pl.pallas_call(
        p_kernel,
        in_specs=[VMEM] * 3,
        out_specs=VMEM,
        out_shape=jax.ShapeDtypeStruct((n, rank, width), F32),
        compiler_params=PARAMS,
        cost_estimate=cost(2 * acts.size * rank * 8, acts.size * 2),
        name="p_chunks",
    )(y_all, acts, e_term)


def merged_kernel(a_ref, g_ref, e_ref, after_ref, hi_ref, lo_ref, a_buf, g_buf, e_buf, a_sems, g_sem, e_sems):
    del after_ref
    blocks, _, block = a_buf.shape

    def loads(i):
        span = pl.ds(i * block, block)
        return (
            pltpu.make_async_copy(a_ref.at[:, span], a_buf.at[i], a_sems.at[i]),
            pltpu.make_async_copy(e_ref.at[span, :], e_buf.at[i], e_sems.at[i]),
        )

    g_load = pltpu.make_async_copy(g_ref, g_buf, g_sem)
    g_load.start()
    for load in loads(0):
        load.start()
    g_load.wait()
    for i in range(blocks):
        for load in loads(i):
            load.wait()
        if i + 1 < blocks:
            for load in loads(i + 1):
                load.start()
        merged = dot(a_buf[i], g_buf[...], 0, 0) + e_buf[i].astype(F32)
        hi, lo = parts_of(merged, 2)
        span = slice(i * block, (i + 1) * block)
        hi_ref[span, :] = hi
        lo_ref[span, :] = lo


def merged_parts(acts_all, grads, error, after):
    tokens, width = acts_all.shape
    cols = grads.shape[1]
    blocks = 2
    block = width // blocks
    shape = jax.ShapeDtypeStruct((width, cols), BF16)
    return pl.pallas_call(
        merged_kernel,
        in_specs=[HBM, HBM, HBM, ANY],
        out_specs=[VMEM, VMEM],
        out_shape=[shape, shape],
        scratch_shapes=[
            pltpu.VMEM((blocks, tokens, block), BF16),
            pltpu.VMEM(grads.shape, BF16),
            pltpu.VMEM((blocks, block, cols), BF16),
            pltpu.SemaphoreType.DMA((blocks,)),
            pltpu.SemaphoreType.DMA,
            pltpu.SemaphoreType.DMA((blocks,)),
        ],
        compiler_params=PARAMS,
        cost_estimate=cost(2 * tokens * width * cols, acts_all.size * 2 + grads.size * 2),
        name="merged_parts",
    )(
        *(
            pltpu.with_memory_space_constraint(x, pltpu.HBM)
            for x in (acts_all, grads, error)
        ),
        after,
    )


def q_kernel(p_ref, hi_ref, lo_ref, out_ref):
    n, rank, width = p_ref.shape
    pieces, rows, _ = out_ref.shape
    total = None
    for s in range(n):
        high, low = parts_of(p_ref[s], 2)
        span = slice(s * width, (s + 1) * width)
        both = dot(jnp.concatenate([high, low], axis=0), hi_ref[span, :])
        term = both[:rank] + (both[rank:] + dot(high, lo_ref[span, :]))
        total = term if total is None else total + term
    for k in range(pieces):
        out_ref[k] = total[k * rows : (k + 1) * rows, :]


def q_pieces(p_all, hi, lo, pieces):
    n, rank, width = p_all.shape
    cols = hi.shape[1]
    return pl.pallas_call(
        q_kernel,
        in_specs=[VMEM] * 3,
        out_specs=VMEM,
        out_shape=jax.ShapeDtypeStruct((pieces, rank // pieces, cols), F32),
        compiler_params=PARAMS,
        cost_estimate=cost(2 * hi.size * rank * 8, hi.size * 4),
        name="q_pieces",
    )(p_all, hi, lo)


def basis_kernel(p_ref, after_ref, inv_ref, basis_ref, stack_ref, full_ref):
    del after_ref
    n, rank, width = p_ref.shape
    for s in range(n):
        full_ref[:, s * width : (s + 1) * width] = p_ref[s]
    p = full_ref[...]
    gram = lax.dot_general(
        p,
        p,
        (((1,), (1,)), ((), ())),
        precision=lax.Precision.HIGHEST,
        preferred_element_type=F32,
    )
    row = lax.broadcasted_iota(jnp.int32, (rank, rank), 0)
    col = lax.broadcasted_iota(jnp.int32, (rank, rank), 1)
    eye = (row == col).astype(F32)
    work = jnp.concatenate([gram, eye], axis=1)
    below = lax.broadcasted_iota(jnp.int32, (rank, 1), 0)
    for j in range(rank - 1):
        pivot = work[j : j + 1, :]
        factor = jnp.where(below > j, work[:, j : j + 1] / pivot[:, j : j + 1], 0.0)
        work = work - factor * pivot
    upper = work[:, :rank]
    pivots = jnp.sum(jnp.where(row == col, upper, 0.0), axis=1, keepdims=True)
    inverse = work[:, rank:] / jnp.sqrt(pivots)
    inv_ref[...] = inverse
    basis = jnp.dot(
        inverse, p, precision=lax.Precision.HIGHEST, preferred_element_type=F32
    )
    basis_ref[...] = basis
    high = basis.astype(BF16).astype(F32)
    low = basis - high
    wide = jnp.concatenate([high, high, low, jnp.zeros_like(low)], axis=0)
    stack_ref[...] = wide.T.astype(BF16)


def basis_of(p_all, after):
    n, rank, width = p_all.shape
    size = n * width
    return pl.pallas_call(
        basis_kernel,
        in_specs=[VMEM, ANY],
        out_specs=[VMEM] * 3,
        out_shape=[
            jax.ShapeDtypeStruct((rank, rank), F32),
            jax.ShapeDtypeStruct((rank, size), F32),
            jax.ShapeDtypeStruct((size, 4 * rank), BF16),
        ],
        scratch_shapes=[pltpu.VMEM((rank, size), F32)],
        compiler_params=PARAMS,
        cost_estimate=cost(4_000_000_000, 4_000_000),
        name="basis",
    )(p_all, after)


def residual_kernel(scale, q_ref, inv_ref, stack_ref, hi_ref, lo_ref, out_ref, factor_ref, raw, factor, out_buf, sems, factor_sem):
    pieces, rows, _ = q_ref.shape
    for k in range(pieces):
        raw[k * rows : (k + 1) * rows, :] = q_ref[k]
    factor[...] = scale * jnp.dot(
        inv_ref[...],
        raw[...],
        precision=lax.Precision.HIGHEST,
        preferred_element_type=F32,
    )
    copies = [pltpu.make_async_copy(factor, factor_ref, factor_sem)]
    copies[0].start()
    high, low = parts_of(factor[...], 2)
    tall = jnp.concatenate([high, low, high, jnp.zeros_like(low)], axis=0)
    blocks = sems.shape[0]
    block = out_ref.shape[0] // blocks
    for i in range(blocks):
        span = pl.ds(i * block, block)
        merged = hi_ref[span, :].astype(F32) + lo_ref[span, :].astype(F32)
        out_buf[span, :] = (merged - dot(stack_ref[span, :], tall)).astype(BF16)
        copies.append(
            pltpu.make_async_copy(out_buf.at[span, :], out_ref.at[span, :], sems.at[i])
        )
        copies[-1].start()
    for copy in copies:
        copy.wait()


def residual_of(q_all, inverse, stack, hi, lo, replicas):
    rank = inverse.shape[0]
    cols = hi.shape[1]
    return pl.pallas_call(
        lambda *refs: residual_kernel(1.0 / replicas, *refs),
        in_specs=[VMEM] * 5,
        out_specs=[HBM, HBM],
        out_shape=[
            jax.ShapeDtypeStruct(hi.shape, BF16),
            jax.ShapeDtypeStruct((rank, cols), F32),
        ],
        scratch_shapes=[
            pltpu.VMEM((rank, cols), F32),
            pltpu.VMEM((rank, cols), F32),
            pltpu.VMEM(hi.shape, BF16),
            pltpu.SemaphoreType.DMA((8,)),
            pltpu.SemaphoreType.DMA,
        ],
        compiler_params=PARAMS,
        name="residual",
    )(q_all, inverse, stack, hi, lo)


def total_kernel(x_ref, out_ref):
    total = x_ref[0]
    for s in range(1, x_ref.shape[0]):
        total = total + x_ref[s]
    for s in range(out_ref.shape[0]):
        out_ref[s] = total


def total_for(x, n):
    return pl.pallas_call(
        total_kernel,
        in_specs=[VMEM],
        out_specs=VMEM,
        out_shape=jax.ShapeDtypeStruct((n,) + x.shape[1:], F32),
        compiler_params=PARAMS,
        cost_estimate=cost(x.size, 4 * x.size),
        name="total",
    )(x)


def per_device(acts, grads_out, error_buffer, prior_q):
    tensor = lax.axis_size("tensor")
    replicas = lax.axis_size("dp")
    side = math.isqrt(replicas)
    along_y = [[y * side + z for y in range(side)] for z in range(side)]
    along_z = [[y * side + z for z in range(side)] for y in range(side)]

    def over_tensor(x):
        return lax.all_to_all(x, "tensor", 0, 0)

    def over_y(x):
        return lax.all_to_all(x, "dp", 0, 0, axis_index_groups=along_y)

    def over_z(x):
        return lax.all_to_all(x, "dp", 0, 0, axis_index_groups=along_z)

    error = error_buffer[0]
    q_t = prior_q.T
    y_mine = y_chunks(q_t, grads_out, tensor)
    late_acts, y_mine = lax.optimization_barrier((acts, y_mine))
    acts_all = lax.all_gather(late_acts, "tensor", axis=0, tiled=True)
    y_all = over_tensor(y_mine)
    p_terms = over_tensor(p_chunks(y_all, acts, error_term(q_t, error)))
    p_row = total_for(over_y(total_for(p_terms, side)), side)
    p_last = total_for(over_z(p_row), tensor)
    p_all = over_tensor(p_last)
    hi, lo = merged_parts(acts_all, grads_out, error, p_last)

    pieces = q_pieces(p_all, hi, lo, side)
    q_sum = total_for(over_z(total_for(over_y(pieces), side)), side)
    q_all = over_y(q_sum)
    inverse, basis, stack = basis_of(p_all, q_sum)
    residual, factor = residual_of(q_all, inverse, stack, hi, lo, replicas)
    return (residual[None], basis.T, factor.T)


def solution(mesh):
    in_specs = (
        P(("dp", "tensor"), None),
        P("dp", "tensor"),
        P("dp", None, "tensor"),
        P("tensor", None),
    )
    out_specs = (P("dp", None, "tensor"), P(), P("tensor", None))
    return jax.shard_map(
        per_device, mesh=mesh, in_specs=in_specs, out_specs=out_specs, check_vma=False
    )
```

```python
import math

import jax
import jax.numpy as jnp
from jax import lax
from jax.experimental import pallas as pl
from jax.experimental.pallas import tpu as pltpu
from jax.sharding import PartitionSpec as P

F32 = jnp.float32
BF16 = jnp.bfloat16
VMEM = pl.BlockSpec(memory_space=pltpu.VMEM)
HBM = pl.BlockSpec(memory_space=pltpu.HBM)
ANY = pl.BlockSpec(memory_space=pl.ANY)
PARAMS = pltpu.CompilerParams(vmem_limit_bytes=32 * 1024 * 1024)
STREAM = pltpu.CompilerParams(vmem_limit_bytes=60 * 1024 * 1024)


def parts_of(x, n):
    out = []
    for _ in range(n):
        part = x.astype(BF16)
        out.append(part)
        x = x - part.astype(F32)
    return out


def dot(a, b, a_dim=1, b_dim=0):
    return lax.dot_general(
        a, b, (((a_dim,), (b_dim,)), ((), ())), preferred_element_type=F32
    )


def cost(flops, moved):
    return pl.CostEstimate(flops=flops, bytes_accessed=moved, transcendentals=0)


def y_kernel(q_ref, g_ref, out_ref, q_buf, g_buf, y_buf, q_sem, g_sems, y_sems):
    n, _, rows = out_ref.shape
    steps = g_sems.shape[0]
    block = g_ref.shape[0] // steps
    q_copy = pltpu.make_async_copy(q_ref, q_buf, q_sem)
    q_copy.start()
    loads, stores = [], []
    for i in range(steps):
        span = pl.ds(i * block, block)
        loads.append(
            pltpu.make_async_copy(g_ref.at[span, :], g_buf.at[span, :], g_sems.at[i])
        )
        loads[i].start()
    q_copy.wait()
    for i in range(steps):
        loads[i].wait()
        y = dot(q_buf[...], g_buf[i * block : (i + 1) * block, :], 1, 1)
        for k in range(block // rows):
            s = i * (block // rows) + k
            y_buf[s] = y[:, k * rows : (k + 1) * rows]
            stores.append(
                pltpu.make_async_copy(y_buf.at[s], out_ref.at[s], y_sems.at[s])
            )
            stores[s].start()
    for store in stores:
        store.wait()


def y_chunks(q_t, grads, n):
    rank, cols = q_t.shape
    rows = grads.shape[0] // n
    return pl.pallas_call(
        y_kernel,
        in_specs=[HBM, HBM],
        out_specs=HBM,
        out_shape=jax.ShapeDtypeStruct((n, rank, rows), F32),
        scratch_shapes=[
            pltpu.VMEM(q_t.shape, BF16),
            pltpu.VMEM(grads.shape, BF16),
            pltpu.VMEM((n, rank, rows), F32),
            pltpu.SemaphoreType.DMA,
            pltpu.SemaphoreType.DMA((2,)),
            pltpu.SemaphoreType.DMA((n,)),
        ],
        compiler_params=STREAM,
        cost_estimate=cost(2 * grads.size * rank * 8, grads.size * 2),
        name="y_chunks",
    )(q_t, grads)


def e_kernel(q_ref, e_ref, out_ref):
    out_ref[...] = dot(q_ref[...], e_ref[...], 1, 1)


def error_term(q_t, error):
    return pl.pallas_call(
        e_kernel,
        in_specs=[VMEM] * 2,
        out_specs=VMEM,
        out_shape=jax.ShapeDtypeStruct((q_t.shape[0], error.shape[0]), F32),
        compiler_params=PARAMS,
        cost_estimate=cost(2 * error.size * 32 * 8, error.size * 2),
        name="error_term",
    )(q_t, error)


def p_kernel(y_ref, acts_ref, e_ref, out_ref):
    n, rank, width = out_ref.shape
    y = y_ref[0]
    for s in range(1, n):
        y = y + y_ref[s]
    stack = jnp.concatenate(parts_of(y, 3), axis=0)
    p = dot(stack, acts_ref[...])
    p = (p[:rank] + e_ref[...]) + (p[rank : 2 * rank] + p[2 * rank :])
    for s in range(n):
        out_ref[s] = p[:, s * width : (s + 1) * width]


def p_chunks(y_all, acts, e_term):
    n, rank, _ = y_all.shape
    width = acts.shape[1] // n
    return pl.pallas_call(
        p_kernel,
        in_specs=[VMEM] * 3,
        out_specs=VMEM,
        out_shape=jax.ShapeDtypeStruct((n, rank, width), F32),
        compiler_params=PARAMS,
        cost_estimate=cost(2 * acts.size * rank * 8, acts.size * 2),
        name="p_chunks",
    )(y_all, acts, e_term)


def merged_kernel(a_ref, g_ref, e_ref, after_ref, hi_ref, lo_ref, a_buf, g_buf, e_buf, a_sems, g_sem, e_sems):
    del after_ref
    blocks, _, block = a_buf.shape

    def loads(i):
        span = pl.ds(i * block, block)
        return (
            pltpu.make_async_copy(a_ref.at[:, span], a_buf.at[i], a_sems.at[i]),
            pltpu.make_async_copy(e_ref.at[span, :], e_buf.at[i], e_sems.at[i]),
        )

    g_load = pltpu.make_async_copy(g_ref, g_buf, g_sem)
    g_load.start()
    for load in loads(0):
        load.start()
    g_load.wait()
    for i in range(blocks):
        for load in loads(i):
            load.wait()
        if i + 1 < blocks:
            for load in loads(i + 1):
                load.start()
        merged = dot(a_buf[i], g_buf[...], 0, 0) + e_buf[i].astype(F32)
        hi, lo = parts_of(merged, 2)
        span = slice(i * block, (i + 1) * block)
        hi_ref[span, :] = hi
        lo_ref[span, :] = lo


def merged_parts(acts_all, grads, error, after):
    tokens, width = acts_all.shape
    cols = grads.shape[1]
    blocks = 2
    block = width // blocks
    shape = jax.ShapeDtypeStruct((width, cols), BF16)
    return pl.pallas_call(
        merged_kernel,
        in_specs=[HBM, HBM, HBM, ANY],
        out_specs=[VMEM, VMEM],
        out_shape=[shape, shape],
        scratch_shapes=[
            pltpu.VMEM((blocks, tokens, block), BF16),
            pltpu.VMEM(grads.shape, BF16),
            pltpu.VMEM((blocks, block, cols), BF16),
            pltpu.SemaphoreType.DMA((blocks,)),
            pltpu.SemaphoreType.DMA,
            pltpu.SemaphoreType.DMA((blocks,)),
        ],
        compiler_params=PARAMS,
        cost_estimate=cost(2 * tokens * width * cols, acts_all.size * 2 + grads.size * 2),
        name="merged_parts",
    )(
        *(
            pltpu.with_memory_space_constraint(x, pltpu.HBM)
            for x in (acts_all, grads, error)
        ),
        after,
    )


def q_kernel(p_ref, hi_ref, lo_ref, out_ref):
    n, rank, width = p_ref.shape
    pieces, rows, _ = out_ref.shape
    total = None
    for s in range(n):
        high, low = parts_of(p_ref[s], 2)
        span = slice(s * width, (s + 1) * width)
        both = dot(jnp.concatenate([high, low], axis=0), hi_ref[span, :])
        term = both[:rank] + (both[rank:] + dot(high, lo_ref[span, :]))
        total = term if total is None else total + term
    for k in range(pieces):
        out_ref[k] = total[k * rows : (k + 1) * rows, :]


def q_pieces(p_all, hi, lo, pieces):
    n, rank, width = p_all.shape
    cols = hi.shape[1]
    return pl.pallas_call(
        q_kernel,
        in_specs=[VMEM] * 3,
        out_specs=VMEM,
        out_shape=jax.ShapeDtypeStruct((pieces, rank // pieces, cols), F32),
        compiler_params=PARAMS,
        cost_estimate=cost(2 * hi.size * rank * 8, hi.size * 4),
        name="q_pieces",
    )(p_all, hi, lo)


def basis_kernel(p_ref, after_ref, inv_ref, basis_ref, stack_ref, full_ref):
    del after_ref
    n, rank, width = p_ref.shape
    for s in range(n):
        full_ref[:, s * width : (s + 1) * width] = p_ref[s]
    p = full_ref[...]
    gram = lax.dot_general(
        p,
        p,
        (((1,), (1,)), ((), ())),
        precision=lax.Precision.HIGHEST,
        preferred_element_type=F32,
    )
    row = lax.broadcasted_iota(jnp.int32, (rank, rank), 0)
    col = lax.broadcasted_iota(jnp.int32, (rank, rank), 1)
    eye = (row == col).astype(F32)
    work = jnp.concatenate([gram, eye], axis=1)
    below = lax.broadcasted_iota(jnp.int32, (rank, 1), 0)
    for j in range(rank - 1):
        pivot = work[j : j + 1, :]
        factor = jnp.where(below > j, work[:, j : j + 1] / pivot[:, j : j + 1], 0.0)
        work = work - factor * pivot
    upper = work[:, :rank]
    pivots = jnp.sum(jnp.where(row == col, upper, 0.0), axis=1, keepdims=True)
    inverse = work[:, rank:] / jnp.sqrt(pivots)
    inv_ref[...] = inverse
    basis = jnp.dot(
        inverse, p, precision=lax.Precision.HIGHEST, preferred_element_type=F32
    )
    basis_ref[...] = basis
    high = basis.astype(BF16).astype(F32)
    low = basis - high
    wide = jnp.concatenate([high, high, low, jnp.zeros_like(low)], axis=0)
    stack_ref[...] = wide.T.astype(BF16)


def basis_of(p_all, after):
    n, rank, width = p_all.shape
    size = n * width
    return pl.pallas_call(
        basis_kernel,
        in_specs=[VMEM, ANY],
        out_specs=[VMEM] * 3,
        out_shape=[
            jax.ShapeDtypeStruct((rank, rank), F32),
            jax.ShapeDtypeStruct((rank, size), F32),
            jax.ShapeDtypeStruct((size, 4 * rank), BF16),
        ],
        scratch_shapes=[pltpu.VMEM((rank, size), F32)],
        compiler_params=PARAMS,
        cost_estimate=cost(4_000_000_000, 4_000_000),
        name="basis",
    )(p_all, after)


def residual_kernel(scale, q_ref, inv_ref, stack_ref, hi_ref, lo_ref, out_ref, factor_ref, raw, factor, out_buf, sems, factor_sem):
    pieces, rows, _ = q_ref.shape
    for k in range(pieces):
        raw[k * rows : (k + 1) * rows, :] = q_ref[k]
    factor[...] = scale * jnp.dot(
        inv_ref[...],
        raw[...],
        precision=lax.Precision.HIGHEST,
        preferred_element_type=F32,
    )
    copies = [pltpu.make_async_copy(factor, factor_ref, factor_sem)]
    copies[0].start()
    high, low = parts_of(factor[...], 2)
    tall = jnp.concatenate([high, low, high, jnp.zeros_like(low)], axis=0)
    blocks = sems.shape[0]
    block = out_ref.shape[0] // blocks
    for i in range(blocks):
        span = pl.ds(i * block, block)
        merged = hi_ref[span, :].astype(F32) + lo_ref[span, :].astype(F32)
        out_buf[span, :] = (merged - dot(stack_ref[span, :], tall)).astype(BF16)
        copies.append(
            pltpu.make_async_copy(out_buf.at[span, :], out_ref.at[span, :], sems.at[i])
        )
        copies[-1].start()
    for copy in copies:
        copy.wait()


def residual_of(q_all, inverse, stack, hi, lo, replicas):
    rank = inverse.shape[0]
    cols = hi.shape[1]
    return pl.pallas_call(
        lambda *refs: residual_kernel(1.0 / replicas, *refs),
        in_specs=[VMEM] * 5,
        out_specs=[HBM, HBM],
        out_shape=[
            jax.ShapeDtypeStruct(hi.shape, BF16),
            jax.ShapeDtypeStruct((rank, cols), F32),
        ],
        scratch_shapes=[
            pltpu.VMEM((rank, cols), F32),
            pltpu.VMEM((rank, cols), F32),
            pltpu.VMEM(hi.shape, BF16),
            pltpu.SemaphoreType.DMA((8,)),
            pltpu.SemaphoreType.DMA,
        ],
        compiler_params=PARAMS,
        name="residual",
    )(q_all, inverse, stack, hi, lo)


def total_kernel(x_ref, out_ref):
    total = x_ref[0]
    for s in range(1, x_ref.shape[0]):
        total = total + x_ref[s]
    for s in range(out_ref.shape[0]):
        out_ref[s] = total


def total_for(x, n):
    return pl.pallas_call(
        total_kernel,
        in_specs=[VMEM],
        out_specs=VMEM,
        out_shape=jax.ShapeDtypeStruct((n,) + x.shape[1:], F32),
        compiler_params=PARAMS,
        cost_estimate=cost(x.size, 4 * x.size),
        name="total",
    )(x)


def per_device(acts, grads_out, error_buffer, prior_q):
    tensor = lax.axis_size("tensor")
    replicas = lax.axis_size("dp")
    side = math.isqrt(replicas)
    both = ("dp", "tensor")

    def line(along, fixed, t):
        pairs = [(i, fixed) if along == 0 else (fixed, i) for i in range(side)]
        return [(y * side + z) * tensor + t for y, z in pairs]

    first, second = (
        [line((t + turn) % 2, k, t) for t in range(tensor) for k in range(side)]
        for turn in range(2)
    )

    def over_tensor(x):
        return lax.all_to_all(x, "tensor", 0, 0)

    def over_first(x):
        return lax.all_to_all(x, both, 0, 0, axis_index_groups=first)

    def over_second(x):
        return lax.all_to_all(x, both, 0, 0, axis_index_groups=second)

    error = error_buffer[0]
    q_t = prior_q.T
    y_mine = y_chunks(q_t, grads_out, tensor)
    late_acts, y_mine = lax.optimization_barrier((acts, y_mine))
    acts_all = lax.all_gather(late_acts, "tensor", axis=0, tiled=True)
    y_all = over_tensor(y_mine)
    p_terms = over_tensor(p_chunks(y_all, acts, error_term(q_t, error)))
    p_row = total_for(over_first(total_for(p_terms, side)), side)
    p_last = total_for(over_second(p_row), tensor)
    p_all = over_tensor(p_last)
    hi, lo = merged_parts(acts_all, grads_out, error, p_last)

    pieces = q_pieces(p_all, hi, lo, side)
    q_sum = total_for(over_second(total_for(over_first(pieces), side)), side)
    q_all = over_first(q_sum)
    inverse, basis, stack = basis_of(p_all, q_sum)
    residual, factor = residual_of(q_all, inverse, stack, hi, lo, replicas)
    return (residual[None], basis.T, factor.T)


def solution(mesh):
    in_specs = (
        P(("dp", "tensor"), None),
        P("dp", "tensor"),
        P("dp", None, "tensor"),
        P("tensor", None),
    )
    out_specs = (P("dp", None, "tensor"), P(), P("tensor", None))
    return jax.shard_map(
        per_device, mesh=mesh, in_specs=in_specs, out_specs=out_specs, check_vma=False
    )
```

```python
import math

import jax
import jax.numpy as jnp
from jax import lax
from jax.experimental import pallas as pl
from jax.experimental.pallas import tpu as pltpu
from jax.sharding import PartitionSpec as P

F32 = jnp.float32
BF16 = jnp.bfloat16
LANES = 128
VMEM = pl.BlockSpec(memory_space=pltpu.VMEM)
HBM = pl.BlockSpec(memory_space=pltpu.HBM)
ANY = pl.BlockSpec(memory_space=pl.ANY)
PARAMS = pltpu.CompilerParams(vmem_limit_bytes=32 * 1024 * 1024)
STREAM = pltpu.CompilerParams(vmem_limit_bytes=60 * 1024 * 1024)


def parts_of(x, n):
    out = []
    for _ in range(n):
        part = x.astype(BF16)
        out.append(part)
        x = x - part.astype(F32)
    return out


def dot(a, b, a_dim=1, b_dim=0):
    return lax.dot_general(
        a, b, (((a_dim,), (b_dim,)), ((), ())), preferred_element_type=F32
    )


def cost(flops, moved):
    return pl.CostEstimate(flops=flops, bytes_accessed=moved, transcendentals=0)


def y_kernel(q_ref, g_ref, out_ref, q_buf, g_buf, y_buf, q_sem, g_sems, y_sems):
    n, _, rows = out_ref.shape
    steps = g_sems.shape[0]
    block = g_ref.shape[0] // steps
    q_copy = pltpu.make_async_copy(q_ref, q_buf, q_sem)
    q_copy.start()
    loads, stores = [], []
    for i in range(steps):
        span = pl.ds(i * block, block)
        loads.append(
            pltpu.make_async_copy(g_ref.at[span, :], g_buf.at[span, :], g_sems.at[i])
        )
        loads[i].start()
    q_copy.wait()
    for i in range(steps):
        loads[i].wait()
        y = dot(q_buf[...], g_buf[i * block : (i + 1) * block, :], 1, 1)
        for k in range(block // rows):
            s = i * (block // rows) + k
            y_buf[s] = y[:, k * rows : (k + 1) * rows]
            stores.append(
                pltpu.make_async_copy(y_buf.at[s], out_ref.at[s], y_sems.at[s])
            )
            stores[s].start()
    for store in stores:
        store.wait()


def y_chunks(q_t, grads, n):
    rank, cols = q_t.shape
    rows = grads.shape[0] // n
    return pl.pallas_call(
        y_kernel,
        in_specs=[HBM, HBM],
        out_specs=HBM,
        out_shape=jax.ShapeDtypeStruct((n, rank, rows), F32),
        scratch_shapes=[
            pltpu.VMEM(q_t.shape, BF16),
            pltpu.VMEM(grads.shape, BF16),
            pltpu.VMEM((n, rank, rows), F32),
            pltpu.SemaphoreType.DMA,
            pltpu.SemaphoreType.DMA((2,)),
            pltpu.SemaphoreType.DMA((n,)),
        ],
        compiler_params=STREAM,
        cost_estimate=cost(2 * grads.size * rank * 8, grads.size * 2),
        name="y_chunks",
    )(q_t, grads)


def e_kernel(q_ref, e_ref, out_ref):
    out_ref[...] = dot(q_ref[...], e_ref[...], 1, 1)


def error_term(q_t, error):
    return pl.pallas_call(
        e_kernel,
        in_specs=[VMEM] * 2,
        out_specs=VMEM,
        out_shape=jax.ShapeDtypeStruct((q_t.shape[0], error.shape[0]), F32),
        compiler_params=PARAMS,
        cost_estimate=cost(2 * error.size * 32 * 8, error.size * 2),
        name="error_term",
    )(q_t, error)


def p_kernel(y_ref, acts_ref, e_ref, out_ref):
    n, rank, width = out_ref.shape
    y = y_ref[0]
    for s in range(1, n):
        y = y + y_ref[s]
    stack = jnp.concatenate(parts_of(y, 3), axis=0)
    p = dot(stack, acts_ref[...])
    p = (p[:rank] + e_ref[...]) + (p[rank : 2 * rank] + p[2 * rank :])
    for s in range(n):
        out_ref[s] = p[:, s * width : (s + 1) * width]


def p_chunks(y_all, acts, e_term):
    n, rank, _ = y_all.shape
    width = acts.shape[1] // n
    return pl.pallas_call(
        p_kernel,
        in_specs=[VMEM] * 3,
        out_specs=VMEM,
        out_shape=jax.ShapeDtypeStruct((n, rank, width), F32),
        compiler_params=PARAMS,
        cost_estimate=cost(2 * acts.size * rank * 8, acts.size * 2),
        name="p_chunks",
    )(y_all, acts, e_term)


def merged_kernel(a_ref, g_ref, e_ref, after_ref, hi_ref, lo_ref, a_buf, g_buf, e_buf, a_sems, g_sem, e_sems):
    del after_ref
    blocks, _, block = a_buf.shape

    def loads(i):
        span = pl.ds(i * block, block)
        return (
            pltpu.make_async_copy(a_ref.at[:, span], a_buf.at[i], a_sems.at[i]),
            pltpu.make_async_copy(e_ref.at[span, :], e_buf.at[i], e_sems.at[i]),
        )

    g_load = pltpu.make_async_copy(g_ref, g_buf, g_sem)
    g_load.start()
    for load in loads(0):
        load.start()
    g_load.wait()
    for i in range(blocks):
        for load in loads(i):
            load.wait()
        if i + 1 < blocks:
            for load in loads(i + 1):
                load.start()
        merged = dot(a_buf[i], g_buf[...], 0, 0) + e_buf[i].astype(F32)
        hi, lo = parts_of(merged, 2)
        span = slice(i * block, (i + 1) * block)
        hi_ref[span, :] = hi
        lo_ref[span, :] = lo


def merged_parts(acts_all, grads, error, after):
    tokens, width = acts_all.shape
    cols = grads.shape[1]
    blocks = 2
    block = width // blocks
    shape = jax.ShapeDtypeStruct((width, cols), BF16)
    return pl.pallas_call(
        merged_kernel,
        in_specs=[HBM, HBM, HBM, ANY],
        out_specs=[VMEM, VMEM],
        out_shape=[shape, shape],
        scratch_shapes=[
            pltpu.VMEM((blocks, tokens, block), BF16),
            pltpu.VMEM(grads.shape, BF16),
            pltpu.VMEM((blocks, block, cols), BF16),
            pltpu.SemaphoreType.DMA((blocks,)),
            pltpu.SemaphoreType.DMA,
            pltpu.SemaphoreType.DMA((blocks,)),
        ],
        compiler_params=PARAMS,
        cost_estimate=cost(2 * tokens * width * cols, acts_all.size * 2 + grads.size * 2),
        name="merged_parts",
    )(
        *(
            pltpu.with_memory_space_constraint(x, pltpu.HBM)
            for x in (acts_all, grads, error)
        ),
        after,
    )


def q_kernel(p_ref, hi_ref, lo_ref, out_ref):
    n, rank, width = p_ref.shape
    pieces, rows, _ = out_ref.shape
    total = None
    for s in range(n):
        high, low = parts_of(p_ref[s], 2)
        span = slice(s * width, (s + 1) * width)
        both = dot(jnp.concatenate([high, low], axis=0), hi_ref[span, :])
        term = both[:rank] + (both[rank:] + dot(high, lo_ref[span, :]))
        total = term if total is None else total + term
    across = total.shape[1] // LANES
    for k in range(pieces):
        r, c = k // across, k % across
        out_ref[k] = total[r * rows : (r + 1) * rows, c * LANES : (c + 1) * LANES]


def q_pieces(p_all, hi, lo, pieces):
    n, rank, width = p_all.shape
    cols = hi.shape[1]
    return pl.pallas_call(
        q_kernel,
        in_specs=[VMEM] * 3,
        out_specs=VMEM,
        out_shape=jax.ShapeDtypeStruct((pieces, rank * cols // (pieces * LANES), LANES), F32),
        compiler_params=PARAMS,
        cost_estimate=cost(2 * hi.size * rank * 8, hi.size * 4),
        name="q_pieces",
    )(p_all, hi, lo)


def basis_kernel(p_ref, after_ref, inv_ref, basis_ref, stack_ref, full_ref):
    del after_ref
    n, rank, width = p_ref.shape
    for s in range(n):
        full_ref[:, s * width : (s + 1) * width] = p_ref[s]
    p = full_ref[...]
    gram = lax.dot_general(
        p,
        p,
        (((1,), (1,)), ((), ())),
        precision=lax.Precision.HIGHEST,
        preferred_element_type=F32,
    )
    row = lax.broadcasted_iota(jnp.int32, (rank, rank), 0)
    col = lax.broadcasted_iota(jnp.int32, (rank, rank), 1)
    eye = (row == col).astype(F32)
    work = jnp.concatenate([gram, eye], axis=1)
    below = lax.broadcasted_iota(jnp.int32, (rank, 1), 0)
    for j in range(rank - 1):
        pivot = work[j : j + 1, :]
        factor = jnp.where(below > j, work[:, j : j + 1] / pivot[:, j : j + 1], 0.0)
        work = work - factor * pivot
    upper = work[:, :rank]
    pivots = jnp.sum(jnp.where(row == col, upper, 0.0), axis=1, keepdims=True)
    inverse = work[:, rank:] / jnp.sqrt(pivots)
    inv_ref[...] = inverse
    basis = jnp.dot(
        inverse, p, precision=lax.Precision.HIGHEST, preferred_element_type=F32
    )
    basis_ref[...] = basis
    high = basis.astype(BF16).astype(F32)
    low = basis - high
    wide = jnp.concatenate([high, high, low, jnp.zeros_like(low)], axis=0)
    stack_ref[...] = wide.T.astype(BF16)


def basis_of(p_all, after):
    n, rank, width = p_all.shape
    size = n * width
    return pl.pallas_call(
        basis_kernel,
        in_specs=[VMEM, ANY],
        out_specs=[VMEM] * 3,
        out_shape=[
            jax.ShapeDtypeStruct((rank, rank), F32),
            jax.ShapeDtypeStruct((rank, size), F32),
            jax.ShapeDtypeStruct((size, 4 * rank), BF16),
        ],
        scratch_shapes=[pltpu.VMEM((rank, size), F32)],
        compiler_params=PARAMS,
        cost_estimate=cost(4_000_000_000, 4_000_000),
        name="basis",
    )(p_all, after)


def residual_kernel(scale, q_ref, inv_ref, stack_ref, hi_ref, lo_ref, out_ref, factor_ref, raw, factor, out_buf, sems, factor_sem):
    pieces, rows, _ = q_ref.shape
    across = raw.shape[1] // LANES
    for k in range(pieces):
        r, c = k // across, k % across
        raw[r * rows : (r + 1) * rows, c * LANES : (c + 1) * LANES] = q_ref[k]
    factor[...] = scale * jnp.dot(
        inv_ref[...],
        raw[...],
        precision=lax.Precision.HIGHEST,
        preferred_element_type=F32,
    )
    copies = [pltpu.make_async_copy(factor, factor_ref, factor_sem)]
    copies[0].start()
    high, low = parts_of(factor[...], 2)
    tall = jnp.concatenate([high, low, high, jnp.zeros_like(low)], axis=0)
    blocks = sems.shape[0]
    block = out_ref.shape[0] // blocks
    for i in range(blocks):
        span = pl.ds(i * block, block)
        merged = hi_ref[span, :].astype(F32) + lo_ref[span, :].astype(F32)
        out_buf[span, :] = (merged - dot(stack_ref[span, :], tall)).astype(BF16)
        copies.append(
            pltpu.make_async_copy(out_buf.at[span, :], out_ref.at[span, :], sems.at[i])
        )
        copies[-1].start()
    for copy in copies:
        copy.wait()


def residual_of(q_all, inverse, stack, hi, lo, replicas):
    rank = inverse.shape[0]
    cols = hi.shape[1]
    return pl.pallas_call(
        lambda *refs: residual_kernel(1.0 / replicas, *refs),
        in_specs=[VMEM] * 5,
        out_specs=[HBM, HBM],
        out_shape=[
            jax.ShapeDtypeStruct(hi.shape, BF16),
            jax.ShapeDtypeStruct((rank, cols), F32),
        ],
        scratch_shapes=[
            pltpu.VMEM((rank, cols), F32),
            pltpu.VMEM((rank, cols), F32),
            pltpu.VMEM(hi.shape, BF16),
            pltpu.SemaphoreType.DMA((8,)),
            pltpu.SemaphoreType.DMA,
        ],
        compiler_params=PARAMS,
        name="residual",
    )(q_all, inverse, stack, hi, lo)


def total_kernel(x_ref, out_ref):
    total = x_ref[0]
    for s in range(1, x_ref.shape[0]):
        total = total + x_ref[s]
    for s in range(out_ref.shape[0]):
        out_ref[s] = total


def total_for(x, n):
    return pl.pallas_call(
        total_kernel,
        in_specs=[VMEM],
        out_specs=VMEM,
        out_shape=jax.ShapeDtypeStruct((n,) + x.shape[1:], F32),
        compiler_params=PARAMS,
        cost_estimate=cost(x.size, 4 * x.size),
        name="total",
    )(x)


def per_device(acts, grads_out, error_buffer, prior_q):
    tensor = lax.axis_size("tensor")
    replicas = lax.axis_size("dp")
    side = math.isqrt(replicas)
    along_y = [[y * side + z for y in range(side)] for z in range(side)]
    along_z = [[y * side + z for z in range(side)] for y in range(side)]

    def over_tensor(x):
        return lax.all_to_all(x, "tensor", 0, 0)

    def over_y(x):
        return lax.all_to_all(x, "dp", 0, 0, axis_index_groups=along_y)

    def over_z(x):
        return lax.all_to_all(x, "dp", 0, 0, axis_index_groups=along_z)

    error = error_buffer[0]
    q_t = prior_q.T
    y_mine = y_chunks(q_t, grads_out, tensor)
    late_acts, y_mine = lax.optimization_barrier((acts, y_mine))
    acts_all = lax.all_gather(late_acts, "tensor", axis=0, tiled=True)
    y_all = over_tensor(y_mine)
    p_terms = over_tensor(p_chunks(y_all, acts, error_term(q_t, error)))
    p_row = total_for(over_y(total_for(p_terms, side)), side)
    p_last = total_for(over_z(p_row), tensor)
    p_all = over_tensor(p_last)
    hi, lo = merged_parts(acts_all, grads_out, error, p_last)

    pieces = q_pieces(p_all, hi, lo, side)
    q_sum = total_for(over_z(total_for(over_y(pieces), side)), side)
    q_all = over_y(q_sum)
    inverse, basis, stack = basis_of(p_all, q_sum)
    residual, factor = residual_of(q_all, inverse, stack, hi, lo, replicas)
    return (residual[None], basis.T, factor.T)


def solution(mesh):
    in_specs = (
        P(("dp", "tensor"), None),
        P("dp", "tensor"),
        P("dp", None, "tensor"),
        P("tensor", None),
    )
    out_specs = (P("dp", None, "tensor"), P(), P("tensor", None))
    return jax.shard_map(
        per_device, mesh=mesh, in_specs=in_specs, out_specs=out_specs, check_vma=False
    )
```

```python
import math

import jax
import jax.numpy as jnp
from jax import lax
from jax.experimental import pallas as pl
from jax.experimental.pallas import tpu as pltpu
from jax.sharding import PartitionSpec as P

F32 = jnp.float32
BF16 = jnp.bfloat16
LANES = 128
VMEM = pl.BlockSpec(memory_space=pltpu.VMEM)
HBM = pl.BlockSpec(memory_space=pltpu.HBM)
ANY = pl.BlockSpec(memory_space=pl.ANY)
PARAMS = pltpu.CompilerParams(vmem_limit_bytes=32 * 1024 * 1024)
STREAM = pltpu.CompilerParams(vmem_limit_bytes=60 * 1024 * 1024)


def parts_of(x, n):
    out = []
    for _ in range(n):
        part = x.astype(BF16)
        out.append(part)
        x = x - part.astype(F32)
    return out


def dot(a, b, a_dim=1, b_dim=0):
    return lax.dot_general(
        a, b, (((a_dim,), (b_dim,)), ((), ())), preferred_element_type=F32
    )


def cost(flops, moved):
    return pl.CostEstimate(flops=flops, bytes_accessed=moved, transcendentals=0)


def y_kernel(q_ref, g_ref, out_ref, q_buf, g_buf, y_buf, q_sem, g_sems, y_sems):
    n, _, rows = out_ref.shape
    steps = g_sems.shape[0]
    block = g_ref.shape[0] // steps
    q_copy = pltpu.make_async_copy(q_ref, q_buf, q_sem)
    q_copy.start()
    loads, stores = [], []
    for i in range(steps):
        span = pl.ds(i * block, block)
        loads.append(
            pltpu.make_async_copy(g_ref.at[span, :], g_buf.at[span, :], g_sems.at[i])
        )
        loads[i].start()
    q_copy.wait()
    for i in range(steps):
        loads[i].wait()
        y = dot(q_buf[...], g_buf[i * block : (i + 1) * block, :], 1, 1)
        for k in range(block // rows):
            s = i * (block // rows) + k
            y_buf[s] = y[:, k * rows : (k + 1) * rows]
            stores.append(
                pltpu.make_async_copy(y_buf.at[s], out_ref.at[s], y_sems.at[s])
            )
            stores[s].start()
    for store in stores:
        store.wait()


def y_chunks(q_t, grads, n):
    rank, cols = q_t.shape
    rows = grads.shape[0] // n
    return pl.pallas_call(
        y_kernel,
        in_specs=[HBM, HBM],
        out_specs=HBM,
        out_shape=jax.ShapeDtypeStruct((n, rank, rows), F32),
        scratch_shapes=[
            pltpu.VMEM(q_t.shape, BF16),
            pltpu.VMEM(grads.shape, BF16),
            pltpu.VMEM((n, rank, rows), F32),
            pltpu.SemaphoreType.DMA,
            pltpu.SemaphoreType.DMA((2,)),
            pltpu.SemaphoreType.DMA((n,)),
        ],
        compiler_params=STREAM,
        cost_estimate=cost(2 * grads.size * rank * 8, grads.size * 2),
        name="y_chunks",
    )(q_t, grads)


def e_kernel(q_ref, e_ref, out_ref):
    out_ref[...] = dot(q_ref[...], e_ref[...], 1, 1)


def error_term(q_t, error):
    return pl.pallas_call(
        e_kernel,
        in_specs=[VMEM] * 2,
        out_specs=VMEM,
        out_shape=jax.ShapeDtypeStruct((q_t.shape[0], error.shape[0]), F32),
        compiler_params=PARAMS,
        cost_estimate=cost(2 * error.size * 32 * 8, error.size * 2),
        name="error_term",
    )(q_t, error)


def p_kernel(y_ref, acts_ref, e_ref, out_ref):
    n, rank, width = out_ref.shape
    y = y_ref[0]
    for s in range(1, n):
        y = y + y_ref[s]
    stack = jnp.concatenate(parts_of(y, 3), axis=0)
    p = dot(stack, acts_ref[...])
    p = (p[:rank] + e_ref[...]) + (p[rank : 2 * rank] + p[2 * rank :])
    for s in range(n):
        out_ref[s] = p[:, s * width : (s + 1) * width]


def p_chunks(y_all, acts, e_term):
    n, rank, _ = y_all.shape
    width = acts.shape[1] // n
    return pl.pallas_call(
        p_kernel,
        in_specs=[VMEM] * 3,
        out_specs=VMEM,
        out_shape=jax.ShapeDtypeStruct((n, rank, width), F32),
        compiler_params=PARAMS,
        cost_estimate=cost(2 * acts.size * rank * 8, acts.size * 2),
        name="p_chunks",
    )(y_all, acts, e_term)


def merged_kernel(a_ref, g_ref, e_ref, after_ref, hi_ref, lo_ref, a_buf, g_buf, e_buf, a_sems, g_sem, e_sems):
    del after_ref
    blocks, _, block = a_buf.shape

    def loads(i):
        span = pl.ds(i * block, block)
        return (
            pltpu.make_async_copy(a_ref.at[:, span], a_buf.at[i], a_sems.at[i]),
            pltpu.make_async_copy(e_ref.at[span, :], e_buf.at[i], e_sems.at[i]),
        )

    g_load = pltpu.make_async_copy(g_ref, g_buf, g_sem)
    g_load.start()
    for load in loads(0):
        load.start()
    g_load.wait()
    for i in range(blocks):
        for load in loads(i):
            load.wait()
        if i + 1 < blocks:
            for load in loads(i + 1):
                load.start()
        merged = dot(a_buf[i], g_buf[...], 0, 0) + e_buf[i].astype(F32)
        hi, lo = parts_of(merged, 2)
        span = slice(i * block, (i + 1) * block)
        hi_ref[span, :] = hi
        lo_ref[span, :] = lo


def merged_parts(acts_all, grads, error, after):
    tokens, width = acts_all.shape
    cols = grads.shape[1]
    blocks = 2
    block = width // blocks
    shape = jax.ShapeDtypeStruct((width, cols), BF16)
    return pl.pallas_call(
        merged_kernel,
        in_specs=[HBM, HBM, HBM, ANY],
        out_specs=[VMEM, VMEM],
        out_shape=[shape, shape],
        scratch_shapes=[
            pltpu.VMEM((blocks, tokens, block), BF16),
            pltpu.VMEM(grads.shape, BF16),
            pltpu.VMEM((blocks, block, cols), BF16),
            pltpu.SemaphoreType.DMA((blocks,)),
            pltpu.SemaphoreType.DMA,
            pltpu.SemaphoreType.DMA((blocks,)),
        ],
        compiler_params=PARAMS,
        cost_estimate=cost(2 * tokens * width * cols, acts_all.size * 2 + grads.size * 2),
        name="merged_parts",
    )(
        *(
            pltpu.with_memory_space_constraint(x, pltpu.HBM)
            for x in (acts_all, grads, error)
        ),
        after,
    )


def q_kernel(p_ref, hi_ref, lo_ref, out_ref):
    n, rank, width = p_ref.shape
    pieces, rows, _ = out_ref.shape
    total = None
    for s in range(n):
        high, low = parts_of(p_ref[s], 2)
        span = slice(s * width, (s + 1) * width)
        both = dot(jnp.concatenate([high, low], axis=0), hi_ref[span, :])
        term = both[:rank] + (both[rank:] + dot(high, lo_ref[span, :]))
        total = term if total is None else total + term
    across = total.shape[1] // LANES
    for k in range(pieces):
        r, c = k // across, k % across
        out_ref[k] = total[r * rows : (r + 1) * rows, c * LANES : (c + 1) * LANES]


def q_pieces(p_all, hi, lo, pieces):
    n, rank, width = p_all.shape
    cols = hi.shape[1]
    return pl.pallas_call(
        q_kernel,
        in_specs=[VMEM] * 3,
        out_specs=VMEM,
        out_shape=jax.ShapeDtypeStruct((pieces, rank * cols // (pieces * LANES), LANES), F32),
        compiler_params=PARAMS,
        cost_estimate=cost(2 * hi.size * rank * 8, hi.size * 4),
        name="q_pieces",
    )(p_all, hi, lo)


def basis_kernel(p_ref, after_ref, inv_ref, basis_ref, stack_ref, full_ref):
    del after_ref
    n, rank, width = p_ref.shape
    for s in range(n):
        full_ref[:, s * width : (s + 1) * width] = p_ref[s]
    p = full_ref[...]
    gram = lax.dot_general(
        p,
        p,
        (((1,), (1,)), ((), ())),
        precision=lax.Precision.HIGHEST,
        preferred_element_type=F32,
    )
    row = lax.broadcasted_iota(jnp.int32, (rank, rank), 0)
    col = lax.broadcasted_iota(jnp.int32, (rank, rank), 1)
    eye = (row == col).astype(F32)
    work = jnp.concatenate([gram, eye], axis=1)
    below = lax.broadcasted_iota(jnp.int32, (rank, 1), 0)
    for j in range(rank - 1):
        pivot = work[j : j + 1, :]
        factor = jnp.where(below > j, work[:, j : j + 1] / pivot[:, j : j + 1], 0.0)
        work = work - factor * pivot
    upper = work[:, :rank]
    pivots = jnp.sum(jnp.where(row == col, upper, 0.0), axis=1, keepdims=True)
    inverse = work[:, rank:] / jnp.sqrt(pivots)
    inv_ref[...] = inverse
    basis = jnp.dot(
        inverse, p, precision=lax.Precision.HIGHEST, preferred_element_type=F32
    )
    basis_ref[...] = basis
    high = basis.astype(BF16).astype(F32)
    low = basis - high
    wide = jnp.concatenate([high, high, low, jnp.zeros_like(low)], axis=0)
    stack_ref[...] = wide.T.astype(BF16)


def basis_of(p_all, after):
    n, rank, width = p_all.shape
    size = n * width
    return pl.pallas_call(
        basis_kernel,
        in_specs=[VMEM, ANY],
        out_specs=[VMEM] * 3,
        out_shape=[
            jax.ShapeDtypeStruct((rank, rank), F32),
            jax.ShapeDtypeStruct((rank, size), F32),
            jax.ShapeDtypeStruct((size, 4 * rank), BF16),
        ],
        scratch_shapes=[pltpu.VMEM((rank, size), F32)],
        compiler_params=PARAMS,
        cost_estimate=cost(4_000_000_000, 4_000_000),
        name="basis",
    )(p_all, after)


def residual_kernel(scale, q_ref, inv_ref, stack_ref, hi_ref, lo_ref, out_ref, factor_ref, raw, factor, out_buf, sems, factor_sem):
    pieces, rows, _ = q_ref.shape
    across = raw.shape[1] // LANES
    for k in range(pieces):
        r, c = k // across, k % across
        raw[r * rows : (r + 1) * rows, c * LANES : (c + 1) * LANES] = q_ref[k]
    factor[...] = scale * jnp.dot(
        inv_ref[...],
        raw[...],
        precision=lax.Precision.HIGHEST,
        preferred_element_type=F32,
    )
    copies = [pltpu.make_async_copy(factor, factor_ref, factor_sem)]
    copies[0].start()
    high, low = parts_of(factor[...], 2)
    tall = jnp.concatenate([high, low, high, jnp.zeros_like(low)], axis=0)
    blocks = sems.shape[0]
    block = out_ref.shape[0] // blocks
    for i in range(blocks):
        span = pl.ds(i * block, block)
        merged = hi_ref[span, :].astype(F32) + lo_ref[span, :].astype(F32)
        out_buf[span, :] = (merged - dot(stack_ref[span, :], tall)).astype(BF16)
        copies.append(
            pltpu.make_async_copy(out_buf.at[span, :], out_ref.at[span, :], sems.at[i])
        )
        copies[-1].start()
    for copy in copies:
        copy.wait()


def residual_of(q_all, inverse, stack, hi, lo, replicas):
    rank = inverse.shape[0]
    cols = hi.shape[1]
    return pl.pallas_call(
        lambda *refs: residual_kernel(1.0 / replicas, *refs),
        in_specs=[VMEM] * 5,
        out_specs=[HBM, HBM],
        out_shape=[
            jax.ShapeDtypeStruct(hi.shape, BF16),
            jax.ShapeDtypeStruct((rank, cols), F32),
        ],
        scratch_shapes=[
            pltpu.VMEM((rank, cols), F32),
            pltpu.VMEM((rank, cols), F32),
            pltpu.VMEM(hi.shape, BF16),
            pltpu.SemaphoreType.DMA((8,)),
            pltpu.SemaphoreType.DMA,
        ],
        compiler_params=PARAMS,
        name="residual",
    )(q_all, inverse, stack, hi, lo)


def total_kernel(x_ref, out_ref):
    total = x_ref[0]
    for s in range(1, x_ref.shape[0]):
        total = total + x_ref[s]
    for s in range(out_ref.shape[0]):
        out_ref[s] = total


def total_for(x, n):
    return pl.pallas_call(
        total_kernel,
        in_specs=[VMEM],
        out_specs=VMEM,
        out_shape=jax.ShapeDtypeStruct((n,) + x.shape[1:], F32),
        compiler_params=PARAMS,
        cost_estimate=cost(x.size, 4 * x.size),
        name="total",
    )(x)


def per_device(acts, grads_out, error_buffer, prior_q):
    tensor = lax.axis_size("tensor")
    replicas = lax.axis_size("dp")
    side = math.isqrt(replicas)
    along_y = [[y * side + z for y in range(side)] for z in range(side)]
    along_z = [[y * side + z for z in range(side)] for y in range(side)]

    def over_tensor(x):
        return lax.all_to_all(x, "tensor", 0, 0)

    def over_y(x):
        return lax.all_to_all(x, "dp", 0, 0, axis_index_groups=along_y)

    def over_z(x):
        return lax.all_to_all(x, "dp", 0, 0, axis_index_groups=along_z)

    error = error_buffer[0]
    q_t = prior_q.T
    y_mine = y_chunks(q_t, grads_out, tensor)
    late_q, y_mine = lax.optimization_barrier((q_t, y_mine))
    e_term = error_term(late_q, error)
    late_acts, e_term = lax.optimization_barrier((acts, e_term))
    acts_all = lax.all_gather(late_acts, "tensor", axis=0, tiled=True)
    y_all = over_tensor(y_mine)
    p_terms = over_tensor(p_chunks(y_all, acts, e_term))
    p_row = total_for(over_y(total_for(p_terms, side)), side)
    p_last = total_for(over_z(p_row), tensor)
    p_all = over_tensor(p_last)
    hi, lo = merged_parts(acts_all, grads_out, error, p_last)

    pieces = q_pieces(p_all, hi, lo, side)
    q_sum = total_for(over_z(total_for(over_y(pieces), side)), side)
    q_all = over_y(q_sum)
    inverse, basis, stack = basis_of(p_all, q_sum)
    residual, factor = residual_of(q_all, inverse, stack, hi, lo, replicas)
    return (residual[None], basis.T, factor.T)


def solution(mesh):
    in_specs = (
        P(("dp", "tensor"), None),
        P("dp", "tensor"),
        P("dp", None, "tensor"),
        P("tensor", None),
    )
    out_specs = (P("dp", None, "tensor"), P(), P("tensor", None))
    return jax.shard_map(
        per_device, mesh=mesh, in_specs=in_specs, out_specs=out_specs, check_vma=False
    )
```
